128 devices in a mesh: hst: 16 (over y, z), chip: 8 (over x, core).
Axes of the slice: x: 4, y: 4, z: 4, core: 2. Of those that a mesh axis runs over, the one named last changes fastest.
Arguments:
- dense_feats: bfloat16 [32768, 13], P(('hst', 'chip')), may hold values from -6 to 6
- labels: int32 [32768], P(('hst', 'chip')), may hold values 0 or 1
- slot_ids: int32 [32768, 26], P(('hst', 'chip')), may hold values from 0 to 2047
- needed_owner: int32 [262144, 1], P(('hst', 'chip')), may hold values from 0 to 127; in each aligned block of 2048 rows (0 to 2047, 2048 to 4095, ...) at most 32 rows name the same one
- needed_local: int32 [262144], P(('hst', 'chip')), may hold values from 0 to 4095
- evicted: int32 [262144], P(('hst', 'chip')), may hold values 0 or 1
- table_rows: bfloat16 [524288, 128], P(('hst', 'chip')), may hold values from -4 to 4
- table_scale: float32 [524288], P(('hst', 'chip')), may hold values from 0.3 to 3
- table_acc: float32 [524288], P(('hst', 'chip')), may hold values from 0.0001 to 0.01
- cross_down: bfloat16 [3341, 512], replicated, may hold values from -0.109375 to 0.109375
- cross_up: bfloat16 [512, 3341], replicated, may hold values from -0.25 to 0.25
- cross_bias: float32 [3341], replicated, may hold values from -3 to 3
- hidden_weight: bfloat16 [3341, 512], replicated, may hold values from -0.109375 to 0.109375
- hidden_bias: float32 [512], replicated, may hold values from -3 to 3
- out_weight: bfloat16 [512], replicated, may hold values from -0.25 to 0.25
Outputs:
- new_rows: bfloat16 [524288, 128], P(('hst', 'chip'))
- new_scale: float32 [524288], P(('hst', 'chip'))
- new_accum: float32 [524288], P(('hst', 'chip'))
- cache_grad: float32 [262144, 128], P(('hst', 'chip'))
- grad_cross_in: float32 [512, 3341], P(('hst', 'chip'))
- grad_hidden_in: float32 [512, 3341], P(('hst', 'chip'))
- grad_cross_out: float32 [512, 3341], P(('hst', 'chip'))
The draws below stay inside these ranges and needn't reach their ends.
Inputs may be any that keep to these rules, and one draw needn't show every extreme that they name: `needed_owner`: among the 2048 slots of one device at most 32 name the same owner, and in every draw some owner is named exactly 32 times by some device.
All inputs are finite; a program needn't handle non-finite values. No bound on the sum of `labels` or of `evicted` on one device may be relied on, other than what follows from the above.
Results may differ from the reference program's by a relative error of at most 0.0099.
Values may be sent and summed in bfloat16 or wider, within the bound.
A program may use at most 192 MiB of HBM per device.

```python
import math
import jax
import jax.numpy as jnp
import numpy as np
from jax import lax

TABLES = 26
E = 128
DENSE = 13
R = 512
H = 512
B_DEV = 256
NEED = 2048
ROW_DEV = 4096
F = 3341
CAP = 32
TOKENS = 32768
TOTAL_NEED = 262144
ROWS = 524288
N_HST = 16
N_CHIP = 8
DEVICES = 128


def plant(result, rng, smallest, largest):
    shape = result.shape
    index_at = [jax.random.randint(jax.random.fold_in(rng, axis), (), 0, shape[axis]) for axis in range(len(shape))]
    result = result.at[tuple(index_at)].set(smallest)
    longest = shape.index(max(shape))
    index_at[longest] = (index_at[longest] + 1) % shape[longest]
    return result.at[tuple(index_at)].set(largest)


def levels(key, shape, cuts, low, largest):
    def one(position, parts):
        draws = jax.random.uniform(jax.random.fold_in(jax.random.fold_in(key, 6), position), (parts,), jnp.float32, low / len(cuts), largest / len(cuts))
        return jnp.repeat(jnp.exp(draws), shape[position] // parts).reshape((-1,) + (1,) * (len(shape) - position - 1))

    gain = one(*cuts[0])
    for cut in cuts[1:]:
        gain = gain * one(*cut)
    return gain


def routed_block(key, own, number, rows, number_of, top, reach, skew):
    sequence = jax.random.permutation(key, number_of)
    packed, common = portions_of(number_of, rows * top, reach, skew, True), portions_of(number_of, rows * top, reach, skew, False)
    places = jnp.arange(number_of)

    def named(tallies, rotation):
        used = int((tallies > 0).sum())
        fixed = max(1, used // 4)
        shifted = fixed + (places - fixed + rotation * (used - fixed)) % max(1, number_of - fixed)
        return jnp.zeros((number_of,), jnp.int32).at[sequence[jnp.where(places < fixed, places, shifted)]].set(jnp.asarray(tallies, jnp.int32))

    tallies = jnp.where(number % 4 == 0, named(packed, number // 4), named(common, number - number // 4 - 1))
    mixed = jax.random.permutation(jax.random.fold_in(own, 3), number_of)
    source_of, sink = mixed[0:number_of // 2 * 2:2], mixed[1:number_of // 2 * 2:2]
    margin = jnp.minimum(tallies[source_of] - 1, reach - tallies[sink]) // 2
    margin = jnp.where((source_of == sequence[0]) | (sink == sequence[0]) | (tallies[sink] == 0), 0, jnp.maximum(margin, 0))
    shifted = jax.random.randint(jax.random.fold_in(own, 4), (number_of // 2,), 0, 1 << 20) % (margin + 1)
    tallies = tallies.at[source_of].add(-shifted).at[sink].add(shifted)
    members = jnp.searchsorted(jnp.cumsum(tallies), jnp.arange(rows * top), side="right").astype(jnp.int32)
    grid = members.reshape(top, rows).T
    grid = grid[jax.random.permutation(jax.random.fold_in(own, 1), rows)]
    rotation = jax.random.randint(jax.random.fold_in(own, 2), (rows, 1), 0, top)
    return jnp.take_along_axis(grid, (jnp.arange(top)[None, :] + rotation) % top, axis=1)


def portions_of(number_of, total, reach, skew, full):
    portions = [(1 << 20) // math.isqrt(grade ** skew) + 1 for grade in range(1, number_of + 1)]
    largest = reach if full else min(reach, max(-(-total // number_of), total * portions[0] // sum(portions)))
    least = 1 if total - largest >= number_of - 1 else 0
    holding, rest = [largest] + [least] * (number_of - 1), total - largest - least * (number_of - 1)
    while rest > 0:
        candidates = [i for i in range(1, number_of) if holding[i] < largest] or [i for i in range(1, number_of) if holding[i] < reach]
        mass, remaining = sum([portions[i] for i in candidates]), rest
        for i in candidates:
            extra = min(reach - holding[i], max(1, remaining * portions[i] // mass), rest)
            holding[i] = holding[i] + extra
            rest = rest - extra
    return np.array(holding)


def noise(stream_key, dims, deviation, limit, split=(), held_as=jnp.bfloat16):
    result = deviation * jax.random.normal(stream_key, dims, jnp.float32)
    if split:
        result = result * levels(stream_key, dims, split, -0.22, 0.18)
    return jnp.clip(result, -limit, limit).astype(held_as)


def setup_inputs(seed: int = 0) -> dict:
    keys = jax.random.split(jax.random.key(seed), 16)
    dense_feats = noise(keys[0], (TOKENS, DENSE), 1.0, 6.0, ((0, 128),))
    labels = plant((jax.random.randint(keys[1], (TOKENS,), 0, 4) < 1).astype(jnp.int32), jax.random.fold_in(keys[1], 1), 0, 1)
    slot_ids = plant(jax.random.randint(keys[2], (TOKENS, TABLES), 0, NEED), jax.random.fold_in(keys[2], 1), 0, NEED - 1).astype(jnp.int32)
    needed_owner_keys = jax.random.split(jax.random.fold_in(keys[3], 1), TOTAL_NEED // NEED)
    needed_owner_turns = jax.random.permutation(jax.random.fold_in(keys[3], 3), TOTAL_NEED // NEED)
    needed_owner = jax.vmap(lambda own, number: routed_block(jax.random.fold_in(keys[3], 2), own, number, NEED, DEVICES, 1, CAP, 2))(needed_owner_keys, needed_owner_turns).reshape((TOTAL_NEED, 1))
    needed_local = plant(jax.random.randint(keys[4], (TOTAL_NEED,), 0, ROW_DEV), jax.random.fold_in(keys[4], 1), 0, ROW_DEV - 1).astype(jnp.int32)
    evicted = plant((jax.random.randint(keys[5], (TOTAL_NEED,), 0, 2) < 1).astype(jnp.int32), jax.random.fold_in(keys[5], 1), 0, 1)
    table_rows = noise(keys[6], (ROWS, E), 1.0, 4.0, ((0, 128),))
    table_scale = jnp.clip(jnp.exp(math.log(3.0) - 2.3025851 * jax.random.uniform(keys[7], (ROWS,), jnp.float32) ** levels(keys[7], (ROWS,), ((0, 128),), -0.2, 0.2)), 0.3, 3.0)
    table_acc = jnp.clip(jnp.exp(math.log(0.01) - 4.6051702 * jax.random.uniform(keys[8], (ROWS,), jnp.float32) ** levels(keys[8], (ROWS,), ((0, 128),), -0.2, 0.2)), 0.0001, 0.01)
    cross_down = noise(keys[9], (F, R), F ** -0.5, 0.109375)
    cross_up = noise(keys[10], (R, F), R ** -0.5, 0.25)
    cross_bias = noise(keys[11], (F,), 0.5, 3.0, (), jnp.float32)
    hidden_weight = noise(keys[12], (F, H), F ** -0.5, 0.109375)
    hidden_bias = noise(keys[13], (H,), 0.5, 3.0, (), jnp.float32)
    out_weight = noise(keys[14], (H,), H ** -0.5, 0.25)
    return dict(dense_feats=dense_feats, labels=labels, slot_ids=slot_ids, needed_owner=needed_owner, needed_local=needed_local, evicted=evicted, table_rows=table_rows, table_scale=table_scale, table_acc=table_acc, cross_down=cross_down, cross_up=cross_up, cross_bias=cross_bias, hidden_weight=hidden_weight, hidden_bias=hidden_bias, out_weight=out_weight)


LEARN_RATE = 0.1
QUANT_TOP = 4.0

def contract_last(left, right):
    return lax.dot_general(left, right, (((1,), (1,)), ((), ())), preferred_element_type=jnp.float32)

def contract_first(left, right):
    return lax.dot_general(left, right, (((0,), (0,)), ((), ())), preferred_element_type=jnp.float32)

def dense_step(base_in, labels, cross_down, cross_up, cross_bias, hidden_weight, hidden_bias, out_weight):
    low_rank = jnp.dot(base_in, cross_down, preferred_element_type=jnp.float32).astype(jnp.bfloat16)
    mixing = jnp.dot(low_rank, cross_up, preferred_element_type=jnp.float32)
    base_wide = base_in.astype(jnp.float32)
    crossed = (base_wide * (mixing + cross_bias[None, :]) + base_wide).astype(jnp.bfloat16)
    preact = jnp.dot(crossed, hidden_weight, preferred_element_type=jnp.float32) + hidden_bias[None, :]
    sig_pre = jax.nn.sigmoid(preact)
    hidden = (preact * sig_pre).astype(jnp.bfloat16)
    logits = jnp.dot(hidden, out_weight, preferred_element_type=jnp.float32)
    grad_logit = jax.nn.sigmoid(logits) - labels.astype(jnp.float32)
    slope = sig_pre * (1.0 + preact * (1.0 - sig_pre))
    grad_hidden = (grad_logit[:, None] * out_weight.astype(jnp.float32)[None, :] * slope).astype(jnp.bfloat16)
    grad_cross = contract_last(grad_hidden, hidden_weight)
    grad_mix = (grad_cross * base_wide).astype(jnp.bfloat16)
    grad_low = contract_last(grad_mix, cross_up).astype(jnp.bfloat16)
    grad_input = grad_cross * (mixing + cross_bias[None, :] + 1.0) + contract_last(grad_low, cross_down)
    return (low_rank, crossed, grad_hidden, grad_mix, grad_low, grad_input)

def reference(dense_feats, labels, slot_ids, needed_owner, needed_local, evicted, table_rows, table_scale, table_acc, cross_down, cross_up, cross_bias, hidden_weight, hidden_bias, out_weight):
    devices = N_HST * N_CHIP
    global_rows = (needed_owner[:, 0] * ROW_DEV + needed_local).astype(jnp.int32)
    fetched = (table_rows[global_rows].astype(jnp.float32) * table_scale[global_rows][:, None]).astype(jnp.bfloat16)
    fetched_dev = fetched.reshape(devices, NEED, E)
    dense_dev = dense_feats.reshape(devices, B_DEV, DENSE)
    labels_dev = labels.reshape(devices, B_DEV)
    slots_dev = slot_ids.reshape(devices, B_DEV, TABLES)

    def one_device(carry, pieces):
        fetched_one, dense_one, labels_one, slots_one = pieces
        embedded = fetched_one[slots_one].reshape(B_DEV, TABLES * E)
        base_in = jnp.concatenate([embedded, dense_one], axis=1)
        low_rank, crossed, grad_hidden, grad_mix, grad_low, grad_input = dense_step(base_in, labels_one, cross_down, cross_up, cross_bias, hidden_weight, hidden_bias, out_weight)
        sum_down = carry[0] + contract_first(grad_low, base_in) / devices
        sum_hidden = carry[1] + contract_first(grad_hidden, crossed) / devices
        sum_up = carry[2] + contract_first(low_rank, grad_mix) / devices
        emb_grad = grad_input[:, :TABLES * E].reshape(B_DEV * TABLES, E)
        slot_grad = jax.ops.segment_sum(emb_grad, slots_one.reshape(-1), num_segments=NEED)
        return ((sum_down, sum_hidden, sum_up), slot_grad)
    init = (jnp.zeros((R, F), jnp.float32), jnp.zeros((H, F), jnp.float32), jnp.zeros((R, F), jnp.float32))
    sums, slot_all = lax.scan(one_device, init, (fetched_dev, dense_dev, labels_dev, slots_dev))
    slot_all = slot_all.reshape(devices * NEED, E)
    evict_wide = evicted.astype(jnp.float32)[:, None]
    cache_grad = slot_all * (1.0 - evict_wide)
    row_grad = jax.ops.segment_sum(slot_all * evict_wide, global_rows, num_segments=ROW_DEV * devices)
    new_accum = table_acc + lax.optimization_barrier(jnp.mean(row_grad * row_grad, axis=1))
    values = table_rows.astype(jnp.float32) * table_scale[:, None] - LEARN_RATE * row_grad / jnp.sqrt(new_accum)[:, None]
    new_scale = (lax.optimization_barrier(jnp.max(jnp.abs(values), axis=1)) + 1e-06) / QUANT_TOP
    new_rows = (values / new_scale[:, None]).astype(jnp.bfloat16)
    return (new_rows, new_scale, new_accum, cache_grad, sums[0], sums[1], sums[2])
```

```python
import functools

import jax
import jax.experimental.pallas as pl
import jax.experimental.pallas.tpu as pltpu
import jax.numpy as jnp
from jax import lax
from jax.sharding import PartitionSpec as P

MESH = pl.DeviceIdType.MESH
LEARN_RATE = 0.1
QUANT_TOP = 4.0


def contract_last(left, right):
    return lax.dot_general(
        left, right, (((1,), (1,)), ((), ())), preferred_element_type=jnp.float32
    )


def contract_first(left, right):
    return lax.dot_general(
        left, right, (((0,), (0,)), ((), ())), preferred_element_type=jnp.float32
    )


def coords():
    host = lax.axis_index("hst")
    chip = lax.axis_index("chip")
    return host // 4, host % 4, chip // 2, chip % 2


def hosts_from(y, z):
    return [((y + d // 4) % 4) * 4 + (z + d % 4) % 4 for d in range(16)]


def chips_from(x, core):
    return [((x + d // 2) % 4) * 2 + (core + d % 2) % 2 for d in range(8)]


def neg_host(d):
    return ((4 - d // 4) % 4) * 4 + (4 - d % 4) % 4


def neg_chip(d):
    return ((4 - d // 2) % 4) * 2 + d % 2


def greet_all(barrier):
    y, z, x, core = coords()
    chips = chips_from(x, core)

    def one(d, _):
        host = ((y + d // 4) % 4) * 4 + (z + d % 4) % 4
        for e in range(8):
            if e == 0:

                @pl.when(d > 0)
                def _():
                    pl.semaphore_signal(barrier, inc=1, device_id=(host, chips[0]), device_id_type=MESH)

            else:
                pl.semaphore_signal(barrier, inc=1, device_id=(host, chips[e]), device_id_type=MESH)
        return 0

    lax.fori_loop(0, 16, one, 0)


def hot(cond):
    return jnp.where(cond, 1.0, 0.0).astype(jnp.bfloat16)


def to_column(row):
    return jnp.broadcast_to(row, (128, 128)).T


def lane_tiles(col, count):
    lane = lax.broadcasted_iota(jnp.int32, col.shape, 1)
    return jnp.concatenate([hot(col == lane + 128 * i) for i in range(count)], axis=1)


def embed_kernel(
    owner_ref,
    local_ref,
    slots_ref,
    rows_ref,
    scale_ref,
    base_ref,
    pos_ref,
    inc_out_ref,
    req,
    inc,
    val,
    ret,
    table2,
    qcol,
    poscol,
    fetched,
    fetched2,
    sidcol,
    req_send,
    req_recv,
    val_send,
    val_recv,
):
    y, z, x, core = coords()
    chips = chips_from(x, core)
    barrier = pltpu.get_barrier_semaphore()
    greet_all(barrier)

    owner = owner_ref[...]
    rel = (
        (((owner >> 5) - y) & 3) * 32
        + (((owner >> 3) - z) & 3) * 8
        + (((owner >> 1) - x) & 3) * 2
        + ((owner - core) & 1)
    )
    sub = lax.broadcasted_iota(jnp.int32, (128, 256), 0)
    upper = hot(
        lax.broadcasted_iota(jnp.int32, (256, 256), 0) < lax.broadcasted_iota(jnp.int32, (256, 256), 1)
    )
    seen = jnp.zeros((128, 1), jnp.float32)
    hi_sum = jnp.zeros((128, 32), jnp.float32)
    lo_sum = jnp.zeros((128, 32), jnp.float32)
    for i in range(8):
        part = rel[:, 256 * i : 256 * i + 256]
        hits = hot(part == sub)
        before = jnp.dot(hits, upper, preferred_element_type=jnp.float32) + seen
        wide = hits.astype(jnp.float32)
        place = jnp.sum(wide * before, axis=0, keepdims=True).astype(jnp.int32)
        seen = seen + jnp.sum(wide, axis=1, keepdims=True)
        pos_ref[:, 256 * i : 256 * i + 256] = part * 32 + place
        code = local_ref[:, 256 * i : 256 * i + 256] + 1
        here = place == lax.broadcasted_iota(jnp.int32, (32, 256), 0)
        hi = jnp.where(here, (code >> 6).astype(jnp.float32), 0.0).astype(jnp.bfloat16)
        lo = jnp.where(here, (code & 63).astype(jnp.float32), 0.0).astype(jnp.bfloat16)
        hi_sum = hi_sum + contract_last(hits, hi)
        lo_sum = lo_sum + contract_last(hits, lo)
    asked = (hi_sum * 64.0 + lo_sum).astype(jnp.int32) - 1
    asked = jnp.concatenate([asked, jnp.full((128, 96), -1, jnp.int32)], axis=1)
    for k in range(128):
        req[k] = asked[k : k + 1, :]
    inc[0] = req[0]

    pl.semaphore_wait(barrier, 127)

    def ask(d, _):
        host = ((y + d // 4) % 4) * 4 + (z + d % 4) % 4
        back = ((4 - d // 4) % 4) * 4 + (4 - d % 4) % 4
        for e in range(8):

            def go():
                pltpu.make_async_remote_copy(
                    src_ref=req.at[d * 8 + e],
                    dst_ref=inc.at[back * 8 + neg_chip(e)],
                    send_sem=req_send,
                    recv_sem=req_recv,
                    device_id=(host, chips[e]),
                    device_id_type=MESH,
                ).start()

            if e == 0:
                pl.when(d > 0)(go)
            else:
                go()
        return 0

    lax.fori_loop(0, 16, ask, 0)

    for i in range(32):
        rows = rows_ref[128 * i : 128 * i + 128, :].astype(jnp.float32)
        col = to_column(scale_ref[i : i + 1, :])
        table2[(i % 8) * 128 : (i % 8) * 128 + 128, (i // 8) * 128 : (i // 8) * 128 + 128] = (
            rows * col
        ).astype(jnp.bfloat16)
    for i in range(16):
        poscol[128 * i : 128 * i + 128, :] = to_column(pos_ref[:, 128 * i : 128 * i + 128])
    ids = jnp.concatenate([slots_ref[...], jnp.zeros((6, 256), jnp.int32)], axis=0)
    ids = jnp.concatenate([ids, jnp.zeros((96, 256), jnp.int32)], axis=0).T
    for t in range(26):
        sidcol[256 * t : 256 * t + 256, :] = jnp.broadcast_to(ids[:, t : t + 1], (256, 128))

    pltpu.make_async_copy(req.at[pl.ds(0, 127)], req.at[pl.ds(0, 127)], req_send).wait()
    pltpu.make_async_copy(inc.at[pl.ds(1, 127)], inc.at[pl.ds(1, 127)], req_recv).wait()
    got = inc[...].reshape(128, 128)
    inc_out_ref[...] = got
    got_t = got.T
    for k in range(128):
        qcol[32 * k : 32 * k + 32, :] = jnp.broadcast_to(got_t[0:32, k : k + 1], (32, 128))

    def serve(d, _):
        host = ((y + d // 4) % 4) * 4 + (z + d % 4) % 4
        back = ((4 - d // 4) % 4) * 4 + (4 - d % 4) % 4
        at = pl.multiple_of(d * 256, 256)
        query = qcol[pl.ds(at, 256), :]
        found = jnp.dot(lane_tiles(query & 1023, 8), table2[...], preferred_element_type=jnp.float32)
        quarter = query >> 10
        out = jnp.zeros((256, 128), jnp.float32)
        for i in range(4):
            out = jnp.where(quarter == i, found[:, 128 * i : 128 * i + 128], out)
        val[pl.ds(at, 256), :] = out.astype(jnp.bfloat16)
        for e in range(8):

            def go():
                pltpu.make_async_remote_copy(
                    src_ref=val.at[pl.ds(pl.multiple_of(at + 32 * e, 32), 32), :],
                    dst_ref=ret.at[pl.ds(pl.multiple_of(back * 256 + 32 * neg_chip(e), 32), 32), :],
                    send_sem=val_send,
                    recv_sem=val_recv.at[back // 4],
                    device_id=(host, chips[e]),
                    device_id_type=MESH,
                ).start()

            if e == 0:
                pl.when(d > 0)(go)
            else:
                go()
        return 0

    lax.fori_loop(0, 16, serve, 0)
    ret[0:32, :] = val[0:32, :]
    for chunk in (0, 3, 2, 1):
        if chunk == 0:
            landed = ret.at[pl.ds(32, 992), :]
        else:
            landed = ret.at[pl.ds(1024 * chunk, 1024), :]
        pltpu.make_async_copy(landed, landed, val_recv.at[chunk]).wait()
        pair = jnp.concatenate(
            [ret[1024 * chunk : 1024 * chunk + 512, :], ret[1024 * chunk + 512 : 1024 * chunk + 1024, :]],
            axis=1,
        )

        def pick(i, _):
            at = pl.multiple_of(i * 256, 256)
            where = poscol[pl.ds(at, 256), :]
            found = jnp.dot(lane_tiles(where & 511, 4), pair, preferred_element_type=jnp.float32)
            half = where >> 9
            if chunk == 0:
                out = jnp.zeros((256, 128), jnp.float32)
            else:
                out = fetched[pl.ds(at, 256), :]
            out = jnp.where(half == 2 * chunk, found[:, :128], out)
            fetched[pl.ds(at, 256), :] = jnp.where(half == 2 * chunk + 1, found[:, 128:], out)
            return 0

        lax.fori_loop(0, 8, pick, 0)
    fetched2[:, 0:128] = fetched[0:1024, :].astype(jnp.bfloat16)
    fetched2[:, 128:256] = fetched[1024:2048, :].astype(jnp.bfloat16)

    def spread(t, _):
        at = pl.multiple_of(t * 256, 256)
        slot = sidcol[pl.ds(at, 256), :]
        found = jnp.dot(lane_tiles(slot & 1023, 8), fetched2[...], preferred_element_type=jnp.float32)
        base_ref[:, pl.ds(pl.multiple_of(t * 128, 128), 128)] = jnp.where(
            slot < 1024, found[:, :128], found[:, 128:]
        ).astype(jnp.bfloat16)
        return 0

    lax.fori_loop(0, 26, spread, 0)
    sent = val.at[pl.ds(32, 4064), :]
    pltpu.make_async_copy(sent, sent, val_send).wait()


def embed(owner, local, slots_t, rows, scale):
    vmem = pl.BlockSpec(memory_space=pltpu.VMEM)
    return pl.pallas_call(
        embed_kernel,
        name="embed",
        out_shape=(
            jax.ShapeDtypeStruct((256, 3328), jnp.bfloat16),
            jax.ShapeDtypeStruct((1, 2048), jnp.int32),
            jax.ShapeDtypeStruct((128, 128), jnp.int32),
        ),
        in_specs=[vmem] * 5,
        out_specs=(vmem,) * 3,
        scratch_shapes=[
            pltpu.VMEM((128, 1, 128), jnp.int32),
            pltpu.VMEM((128, 1, 128), jnp.int32),
            pltpu.VMEM((4096, 128), jnp.bfloat16),
            pltpu.VMEM((4096, 128), jnp.bfloat16),
            pltpu.VMEM((1024, 512), jnp.bfloat16),
            pltpu.VMEM((4096, 128), jnp.int32),
            pltpu.VMEM((2048, 128), jnp.int32),
            pltpu.VMEM((2048, 128), jnp.float32),
            pltpu.VMEM((1024, 256), jnp.bfloat16),
            pltpu.VMEM((6656, 128), jnp.int32),
            pltpu.SemaphoreType.DMA,
            pltpu.SemaphoreType.DMA,
            pltpu.SemaphoreType.DMA,
            pltpu.SemaphoreType.DMA((4,)),
        ],
        compiler_params=pltpu.CompilerParams(
            collective_id=0, has_side_effects=True, vmem_limit_bytes=48 * 2**20
        ),
    )(owner, local, slots_t, rows, scale)


def send_requests(requests):
    return lax.all_to_all(requests, ("hst", "chip"), split_axis=0, concat_axis=0, tiled=True)


def send_values(served):
    return lax.all_to_all(served, ("hst", "chip"), split_axis=0, concat_axis=0, tiled=True)


def send_grads(outgoing):
    return lax.all_to_all(outgoing, ("hst", "chip"), split_axis=0, concat_axis=0, tiled=True)


def dense_step(
    base_in, labels, cross_down, cross_up, cross_bias, hidden_weight, hidden_bias, out_weight
):
    low_rank = jnp.dot(base_in, cross_down, preferred_element_type=jnp.float32).astype(jnp.bfloat16)
    mixing = jnp.dot(low_rank, cross_up, preferred_element_type=jnp.float32)
    base_wide = base_in.astype(jnp.float32)
    crossed = (base_wide * (mixing + cross_bias[None, :]) + base_wide).astype(jnp.bfloat16)
    preact = (
        jnp.dot(crossed, hidden_weight, preferred_element_type=jnp.float32) + hidden_bias[None, :]
    )
    sig_pre = jax.nn.sigmoid(preact)
    hidden = (preact * sig_pre).astype(jnp.bfloat16)
    logits = jnp.dot(hidden, out_weight, preferred_element_type=jnp.float32)
    grad_logit = jax.nn.sigmoid(logits) - labels.astype(jnp.float32)
    slope = sig_pre * (1.0 + preact * (1.0 - sig_pre))
    grad_hidden = (grad_logit[:, None] * out_weight.astype(jnp.float32)[None, :] * slope).astype(
        jnp.bfloat16
    )
    grad_cross = contract_last(grad_hidden, hidden_weight)
    grad_mix = (grad_cross * base_wide).astype(jnp.bfloat16)
    grad_low = contract_last(grad_mix, cross_up).astype(jnp.bfloat16)
    grad_input = grad_cross * (mixing + cross_bias[None, :] + 1.0) + contract_last(
        grad_low, cross_down
    )
    return (low_rank, crossed, grad_hidden, grad_mix, grad_low, grad_input)


def on_device(
    dense_feats,
    labels,
    slot_ids,
    needed_owner,
    needed_local,
    evicted,
    table_rows,
    table_scale,
    table_acc,
    cross_down,
    cross_up,
    cross_bias,
    hidden_weight,
    hidden_bias,
    out_weight,
):
    n_host = lax.axis_size("hst")
    n_chip = lax.axis_size("chip")
    devices = n_host * n_chip
    owners = needed_owner[:, 0]
    need_rows = owners.shape[0]
    capacity = 2 * need_rows // devices
    emb_width = table_rows.shape[1]
    batch_rows = dense_feats.shape[0]
    owner_hits = (owners[:, None] == jnp.arange(devices, dtype=jnp.int32)[None, :]).astype(
        jnp.int32
    )
    places = jnp.sum(jnp.cumsum(owner_hits, axis=0) * owner_hits, axis=1) - 1
    requests = jnp.full((devices, capacity), -1, jnp.int32).at[owners, places].set(needed_local)
    incoming = send_requests(requests)
    row_index = jnp.where(incoming >= 0, incoming, 0)
    embedded, _, _ = embed(
        owners.reshape(1, -1),
        needed_local.reshape(1, -1),
        slot_ids.T,
        table_rows,
        table_scale.reshape(32, 128),
    )
    base_in = jnp.concatenate([embedded, dense_feats], axis=1)
    low_rank, crossed, grad_hidden, grad_mix, grad_low, grad_input = dense_step(
        base_in, labels, cross_down, cross_up, cross_bias, hidden_weight, hidden_bias, out_weight
    )
    emb_cols = embedded.shape[1]
    emb_grad = grad_input[:, :emb_cols].reshape(-1, emb_width)
    slot_grad = jax.ops.segment_sum(emb_grad, slot_ids.reshape(-1), num_segments=need_rows)
    evict_wide = evicted.astype(jnp.float32)[:, None]
    cache_grad = slot_grad * (1.0 - evict_wide)
    outgoing = (
        jnp.zeros((devices, capacity, emb_width), jnp.float32)
        .at[owners, places]
        .set(slot_grad * evict_wide)
    )
    received = send_grads(outgoing)
    row_grad = jax.ops.segment_sum(
        received.reshape(-1, emb_width), row_index.reshape(-1), num_segments=table_rows.shape[0]
    )
    new_accum = table_acc + jnp.mean(row_grad * row_grad, axis=1)
    values = (
        table_rows.astype(jnp.float32) * table_scale[:, None]
        - LEARN_RATE * row_grad / jnp.sqrt(new_accum)[:, None]
    )
    new_scale = (jnp.max(jnp.abs(values), axis=1) + 1e-06) / QUANT_TOP
    new_rows = (values / new_scale[:, None]).astype(jnp.bfloat16)
    partials = (
        contract_first(grad_low, base_in) / devices,
        contract_first(grad_hidden, crossed) / devices,
        contract_first(low_rank, grad_mix) / devices,
    )
    grad_down, grad_hid, grad_up = (
        lax.psum_scatter(partials[0], ("hst", "chip"), scatter_dimension=0, tiled=True),
        lax.psum_scatter(partials[1], ("hst", "chip"), scatter_dimension=0, tiled=True),
        lax.psum_scatter(partials[2], ("hst", "chip"), scatter_dimension=0, tiled=True),
    )
    return (new_rows, new_scale, new_accum, cache_grad, grad_down, grad_hid, grad_up)


def solution(mesh):
    placed = (
        P(("hst", "chip"), None),
        P(("hst", "chip")),
        P(("hst", "chip"), None),
        P(("hst", "chip"), None),
        P(("hst", "chip")),
        P(("hst", "chip")),
        P(("hst", "chip"), None),
        P(("hst", "chip")),
        P(("hst", "chip")),
        P(),
        P(),
        P(),
        P(),
        P(),
        P(),
    )
    return jax.shard_map(
        on_device,
        mesh=mesh,
        in_specs=placed,
        out_specs=(
            P(("hst", "chip"), None),
            P(("hst", "chip")),
            P(("hst", "chip")),
            P(("hst", "chip"), None),
            P(("hst", "chip"), None),
            P(("hst", "chip"), None),
            P(("hst", "chip"), None),
        ),
        check_vma=False,
    )
```

```python
import functools

import jax
import jax.experimental.pallas as pl
import jax.experimental.pallas.tpu as pltpu
import jax.numpy as jnp
from jax import lax
from jax.sharding import PartitionSpec as P

MESH = pl.DeviceIdType.MESH
LEARN_RATE = 0.1
QUANT_TOP = 4.0


def contract_last(left, right):
    return lax.dot_general(
        left, right, (((1,), (1,)), ((), ())), preferred_element_type=jnp.float32
    )


def contract_first(left, right):
    return lax.dot_general(
        left, right, (((0,), (0,)), ((), ())), preferred_element_type=jnp.float32
    )


def coords():
    host = lax.axis_index("hst")
    chip = lax.axis_index("chip")
    return host // 4, host % 4, chip // 2, chip % 2


def hosts_from(y, z):
    return [((y + d // 4) % 4) * 4 + (z + d % 4) % 4 for d in range(16)]


def chips_from(x, core):
    return [((x + d // 2) % 4) * 2 + (core + d % 2) % 2 for d in range(8)]


def neg_host(d):
    return ((4 - d // 4) % 4) * 4 + (4 - d % 4) % 4


def neg_chip(d):
    return ((4 - d // 2) % 4) * 2 + d % 2


def greet_all(barrier):
    y, z, x, core = coords()
    chips = chips_from(x, core)

    def one(d, _):
        host = ((y + d // 4) % 4) * 4 + (z + d % 4) % 4
        for e in range(8):
            if e == 0:

                @pl.when(d > 0)
                def _():
                    pl.semaphore_signal(barrier, inc=1, device_id=(host, chips[0]), device_id_type=MESH)

            else:
                pl.semaphore_signal(barrier, inc=1, device_id=(host, chips[e]), device_id_type=MESH)
        return 0

    lax.fori_loop(0, 16, one, 0)


def hot(cond):
    return jnp.where(cond, 1.0, 0.0).astype(jnp.bfloat16)


def to_column(row):
    return jnp.broadcast_to(row, (128, 128)).T


def lane_tiles(col, count):
    lane = lax.broadcasted_iota(jnp.int32, col.shape, 1)
    return jnp.concatenate([hot(col == lane + 128 * i) for i in range(count)], axis=1)


def embed_kernel(
    owner_ref,
    local_ref,
    slots_ref,
    rows_ref,
    scale_ref,
    feats_ref,
    base_ref,
    pos_ref,
    inc_out_ref,
    req,
    inc,
    val,
    ret,
    table2,
    qcol,
    poscol,
    fetched,
    fetched2,
    sidcol,
    req_send,
    req_recv,
    val_send,
    val_recv,
):
    y, z, x, core = coords()
    chips = chips_from(x, core)
    barrier = pltpu.get_barrier_semaphore()
    greet_all(barrier)

    owner = owner_ref[...]
    rel = (
        (((owner >> 5) - y) & 3) * 32
        + (((owner >> 3) - z) & 3) * 8
        + (((owner >> 1) - x) & 3) * 2
        + ((owner - core) & 1)
    )
    sub = lax.broadcasted_iota(jnp.int32, (128, 256), 0)
    upper = hot(
        lax.broadcasted_iota(jnp.int32, (256, 256), 0) < lax.broadcasted_iota(jnp.int32, (256, 256), 1)
    )
    seen = jnp.zeros((128, 1), jnp.float32)
    hi_sum = jnp.zeros((128, 32), jnp.float32)
    lo_sum = jnp.zeros((128, 32), jnp.float32)
    for i in range(8):
        part = rel[:, 256 * i : 256 * i + 256]
        hits = hot(part == sub)
        before = jnp.dot(hits, upper, preferred_element_type=jnp.float32) + seen
        wide = hits.astype(jnp.float32)
        place = jnp.sum(wide * before, axis=0, keepdims=True).astype(jnp.int32)
        seen = seen + jnp.sum(wide, axis=1, keepdims=True)
        pos_ref[:, 256 * i : 256 * i + 256] = part * 32 + place
        code = local_ref[:, 256 * i : 256 * i + 256] + 1
        here = place == lax.broadcasted_iota(jnp.int32, (32, 256), 0)
        hi = jnp.where(here, (code >> 6).astype(jnp.float32), 0.0).astype(jnp.bfloat16)
        lo = jnp.where(here, (code & 63).astype(jnp.float32), 0.0).astype(jnp.bfloat16)
        hi_sum = hi_sum + contract_last(hits, hi)
        lo_sum = lo_sum + contract_last(hits, lo)
    asked = (hi_sum * 64.0 + lo_sum).astype(jnp.int32) - 1
    asked = jnp.concatenate([asked, jnp.full((128, 96), -1, jnp.int32)], axis=1)
    for k in range(128):
        req[k] = asked[k : k + 1, :]
    inc[0] = req[0]

    pl.semaphore_wait(barrier, 127)

    def ask(d, _):
        host = ((y + d // 4) % 4) * 4 + (z + d % 4) % 4
        back = ((4 - d // 4) % 4) * 4 + (4 - d % 4) % 4
        for e in range(8):

            def go():
                pltpu.make_async_remote_copy(
                    src_ref=req.at[d * 8 + e],
                    dst_ref=inc.at[back * 8 + neg_chip(e)],
                    send_sem=req_send,
                    recv_sem=req_recv,
                    device_id=(host, chips[e]),
                    device_id_type=MESH,
                ).start()

            if e == 0:
                pl.when(d > 0)(go)
            else:
                go()
        return 0

    lax.fori_loop(0, 16, ask, 0)

    for i in range(32):
        rows = rows_ref[128 * i : 128 * i + 128, :].astype(jnp.float32)
        col = to_column(scale_ref[i : i + 1, :])
        table2[(i % 8) * 128 : (i % 8) * 128 + 128, (i // 8) * 128 : (i // 8) * 128 + 128] = (
            rows * col
        ).astype(jnp.bfloat16)
    for i in range(16):
        poscol[128 * i : 128 * i + 128, :] = to_column(pos_ref[:, 128 * i : 128 * i + 128])
    ids = jnp.concatenate([slots_ref[...], jnp.zeros((6, 256), jnp.int32)], axis=0)
    ids = jnp.concatenate([ids, jnp.zeros((96, 256), jnp.int32)], axis=0).T
    for t in range(26):
        sidcol[256 * t : 256 * t + 256, :] = jnp.broadcast_to(ids[:, t : t + 1], (256, 128))

    pltpu.make_async_copy(req.at[pl.ds(0, 127)], req.at[pl.ds(0, 127)], req_send).wait()
    pltpu.make_async_copy(inc.at[pl.ds(1, 127)], inc.at[pl.ds(1, 127)], req_recv).wait()
    got = inc[...].reshape(128, 128)
    inc_out_ref[...] = got
    got_t = got.T
    for k in range(128):
        qcol[32 * k : 32 * k + 32, :] = jnp.broadcast_to(got_t[0:32, k : k + 1], (32, 128))

    def serve(d, _):
        host = ((y + d // 4) % 4) * 4 + (z + d % 4) % 4
        back = ((4 - d // 4) % 4) * 4 + (4 - d % 4) % 4
        at = pl.multiple_of(d * 256, 256)
        query = qcol[pl.ds(at, 256), :]
        found = jnp.dot(lane_tiles(query & 1023, 8), table2[...], preferred_element_type=jnp.float32)
        quarter = query >> 10
        out = jnp.zeros((256, 128), jnp.float32)
        for i in range(4):
            out = jnp.where(quarter == i, found[:, 128 * i : 128 * i + 128], out)
        val[pl.ds(at, 256), :] = out.astype(jnp.bfloat16)
        for e in range(8):

            def go():
                pltpu.make_async_remote_copy(
                    src_ref=val.at[pl.ds(pl.multiple_of(at + 32 * e, 32), 32), :],
                    dst_ref=ret.at[pl.ds(pl.multiple_of(back * 256 + 32 * neg_chip(e), 32), 32), :],
                    send_sem=val_send,
                    recv_sem=val_recv.at[back // 4],
                    device_id=(host, chips[e]),
                    device_id_type=MESH,
                ).start()

            if e == 0:
                pl.when(d > 0)(go)
            else:
                go()
        return 0

    lax.fori_loop(0, 16, serve, 0)
    ret[0:32, :] = val[0:32, :]
    for chunk in (0, 3, 2, 1):
        if chunk == 0:
            landed = ret.at[pl.ds(32, 992), :]
        else:
            landed = ret.at[pl.ds(1024 * chunk, 1024), :]
        pltpu.make_async_copy(landed, landed, val_recv.at[chunk]).wait()
        pair = jnp.concatenate(
            [ret[1024 * chunk : 1024 * chunk + 512, :], ret[1024 * chunk + 512 : 1024 * chunk + 1024, :]],
            axis=1,
        )

        def pick(i, _):
            at = pl.multiple_of(i * 256, 256)
            where = poscol[pl.ds(at, 256), :]
            found = jnp.dot(lane_tiles(where & 511, 4), pair, preferred_element_type=jnp.float32)
            half = where >> 9
            if chunk == 0:
                out = jnp.zeros((256, 128), jnp.float32)
            else:
                out = fetched[pl.ds(at, 256), :]
            out = jnp.where(half == 2 * chunk, found[:, :128], out)
            fetched[pl.ds(at, 256), :] = jnp.where(half == 2 * chunk + 1, found[:, 128:], out)
            return 0

        lax.fori_loop(0, 8, pick, 0)
    fetched2[:, 0:128] = fetched[0:1024, :].astype(jnp.bfloat16)
    fetched2[:, 128:256] = fetched[1024:2048, :].astype(jnp.bfloat16)

    def spread(t, _):
        at = pl.multiple_of(t * 256, 256)
        slot = sidcol[pl.ds(at, 256), :]
        found = jnp.dot(lane_tiles(slot & 1023, 8), fetched2[...], preferred_element_type=jnp.float32)
        base_ref[:, pl.ds(pl.multiple_of(t * 128, 128), 128)] = jnp.where(
            slot < 1024, found[:, :128], found[:, 128:]
        ).astype(jnp.bfloat16)
        return 0

    lax.fori_loop(0, 26, spread, 0)
    base_ref[:, 3328:3584] = feats_ref[...]
    sent = val.at[pl.ds(32, 4064), :]
    pltpu.make_async_copy(sent, sent, val_send).wait()


def embed(owner, local, slots_t, rows, scale, feats):
    vmem = pl.BlockSpec(memory_space=pltpu.VMEM)
    return pl.pallas_call(
        embed_kernel,
        name="embed",
        out_shape=(
            jax.ShapeDtypeStruct((256, 3584), jnp.bfloat16),
            jax.ShapeDtypeStruct((1, 2048), jnp.int32),
            jax.ShapeDtypeStruct((128, 128), jnp.int32),
        ),
        in_specs=[vmem] * 6,
        out_specs=(vmem,) * 3,
        scratch_shapes=[
            pltpu.VMEM((128, 1, 128), jnp.int32),
            pltpu.VMEM((128, 1, 128), jnp.int32),
            pltpu.VMEM((4096, 128), jnp.bfloat16),
            pltpu.VMEM((4096, 128), jnp.bfloat16),
            pltpu.VMEM((1024, 512), jnp.bfloat16),
            pltpu.VMEM((4096, 128), jnp.int32),
            pltpu.VMEM((2048, 128), jnp.int32),
            pltpu.VMEM((2048, 128), jnp.float32),
            pltpu.VMEM((1024, 256), jnp.bfloat16),
            pltpu.VMEM((6656, 128), jnp.int32),
            pltpu.SemaphoreType.DMA,
            pltpu.SemaphoreType.DMA,
            pltpu.SemaphoreType.DMA,
            pltpu.SemaphoreType.DMA((4,)),
        ],
        compiler_params=pltpu.CompilerParams(
            collective_id=0, has_side_effects=True, vmem_limit_bytes=48 * 2**20
        ),
    )(owner, local, slots_t, rows, scale, feats)


def dense_kernel(
    base_ref,
    labels_ref,
    down_hbm,
    up_hbm,
    hid_hbm,
    tails_ref,
    bias_ref,
    hid_bias_ref,
    out_w_ref,
    grad_ref,
    crossed_ref,
    mix_ref,
    low_ref,
    grad_hid_ref,
    grad_low_ref,
    down,
    up,
    hid,
    factor,
    sems,
):
    copies = []
    for i, (src, dst) in enumerate(((down_hbm, down), (up_hbm, up), (hid_hbm, hid))):
        copy = pltpu.make_async_copy(
            src.at[pl.ds(0, 3328), :], dst.at[pl.ds(0, 3328), :], sems.at[i]
        )
        copy.start()
        copies.append(copy)
        dst[3328:3584, :] = tails_ref[:, 512 * i : 512 * i + 512]
    copies[0].wait()
    low_ref[...] = jnp.dot(base_ref[...], down[...], preferred_element_type=jnp.float32).astype(
        jnp.bfloat16
    )
    copies[1].wait()

    def cross(j, _):
        at = pl.multiple_of(j * 256, 256)
        cols = pl.ds(at, 256)
        mixing = contract_last(low_ref[...], up[cols, :]) + bias_ref[:, cols]
        base = base_ref[:, cols].astype(jnp.float32)
        crossed_ref[:, cols] = (base * mixing + base).astype(jnp.bfloat16)
        factor[:, cols] = mixing + 1.0
        return 0

    lax.fori_loop(0, 14, cross, 0)
    copies[2].wait()
    preact = (
        jnp.dot(crossed_ref[...], hid[...], preferred_element_type=jnp.float32) + hid_bias_ref[...]
    )
    sig = jax.nn.sigmoid(preact)
    hidden = (preact * sig).astype(jnp.bfloat16).astype(jnp.float32)
    out_w = out_w_ref[...]
    logits = jnp.sum(hidden * out_w, axis=1, keepdims=True)
    labels = jnp.concatenate(
        [to_column(labels_ref[:, 0:128]), to_column(labels_ref[:, 128:256])], axis=0
    )[:, 0:1]
    grad_logit = jax.nn.sigmoid(logits) - labels
    grad_hid_ref[...] = (grad_logit * out_w * (sig * (1.0 + preact * (1.0 - sig)))).astype(
        jnp.bfloat16
    )

    def back(j, _):
        at = pl.multiple_of(j * 256, 256)
        cols = pl.ds(at, 256)
        grad_cross = contract_last(grad_hid_ref[...], hid[cols, :])
        mix_ref[:, cols] = (grad_cross * base_ref[:, cols].astype(jnp.float32)).astype(jnp.bfloat16)
        factor[:, cols] = grad_cross * factor[:, cols]
        return 0

    lax.fori_loop(0, 14, back, 0)
    grad_low_ref[...] = jnp.dot(mix_ref[...], up[...], preferred_element_type=jnp.float32).astype(
        jnp.bfloat16
    )

    def last(j, _):
        at = pl.multiple_of(j * 256, 256)
        cols = pl.ds(at, 256)
        grad = factor[:, cols] + contract_last(grad_low_ref[...], down[cols, :])
        grad_ref[:, cols] = grad.astype(jnp.bfloat16)
        return 0

    lax.fori_loop(0, 13, last, 0)


def dense(base, labels, down, up_t, hid, tails, bias, hid_bias, out_w):
    vmem = pl.BlockSpec(memory_space=pltpu.VMEM)
    anywhere = pl.BlockSpec(memory_space=pl.ANY)
    wide = jax.ShapeDtypeStruct((256, 3584), jnp.bfloat16)
    thin = jax.ShapeDtypeStruct((256, 512), jnp.bfloat16)
    return pl.pallas_call(
        dense_kernel,
        name="dense",
        out_shape=(jax.ShapeDtypeStruct((256, 3328), jnp.bfloat16), wide, wide, thin, thin, thin),
        in_specs=[vmem, vmem, anywhere, anywhere, anywhere, vmem, vmem, vmem, vmem],
        out_specs=(vmem,) * 6,
        scratch_shapes=[
            pltpu.VMEM((3584, 512), jnp.bfloat16),
            pltpu.VMEM((3584, 512), jnp.bfloat16),
            pltpu.VMEM((3584, 512), jnp.bfloat16),
            pltpu.VMEM((256, 3584), jnp.float32),
            pltpu.SemaphoreType.DMA((3,)),
        ],
        compiler_params=pltpu.CompilerParams(vmem_limit_bytes=48 * 2**20),
        cost_estimate=pl.CostEstimate(
            flops=6 * 2 * 256 * 3584 * 512, bytes_accessed=18 * 2**20, transcendentals=0
        ),
    )(base, labels, down, up_t, hid, tails, bias, hid_bias, out_w)


AXES = (("y", "z", "x"), ("z", "x", "y"), ("x", "y", "z"))
LEFT_OF = (0, 1, 2)


def row_order(array, me):
    row = lax.broadcasted_iota(jnp.int32, (512, 512), 0)
    at = {"core": (me["core"] + (row >> 8)) & 1}
    for stage, axis in enumerate(AXES[array]):
        at[axis] = (me[axis] + (row >> (6 - 2 * stage))) & 3
    source = (at["y"] * 32 + at["z"] * 8 + at["x"] * 2 + at["core"]) * 4 + (row & 3)
    return hot(source == lax.broadcasted_iota(jnp.int32, (512, 512), 1))


def shifted(me, axis, step):
    to = dict(me)
    to[axis] = (me[axis] + step) % 4
    return (to["y"] * 4 + to["z"], to["x"] * 2 + to["core"])


def update_kernel(
    grad_ref,
    base_ref,
    crossed_ref,
    mix_ref,
    low_ref,
    grad_hid_ref,
    grad_low_ref,
    pos_ref,
    inc_ref,
    slots_ref,
    evict_ref,
    rows_ref,
    scale_ref,
    acc_ref,
    new_rows_ref,
    new_scale_ref,
    new_acc_ref,
    cache_ref,
    out_down_ref,
    out_hid_ref,
    out_up_ref,
    split,
    placed,
    out,
    rcv,
    spread,
    mine,
    theirs,
    lefts,
    rights,
    part,
    first,
    second_src,
    second,
    third_src,
    third,
    pair_send,
    pair_recv,
    grad_send,
    grad_recv,
    sum_send,
    sum_recv,
):
    y, z, x, core = coords()
    me = {"y": y, "z": z, "x": x, "core": core}
    chips = chips_from(x, core)
    barrier = pltpu.get_barrier_semaphore()
    greet_all(barrier)

    ids = jnp.concatenate([slots_ref[...], jnp.zeros((102, 256), jnp.int32)], axis=0).T
    for t in range(26):
        half = jnp.broadcast_to(ids[:, t : t + 1] >> 10, (256, 128))
        grad = grad_ref[:, 128 * t : 128 * t + 128].astype(jnp.float32)
        split[256 * t : 256 * t + 256, 0:128] = jnp.where(half == 0, grad, 0.0).astype(jnp.bfloat16)
        split[256 * t : 256 * t + 256, 128:256] = jnp.where(half == 1, grad, 0.0).astype(
            jnp.bfloat16
        )
    factors = (grad_low_ref, grad_hid_ref, low_ref)
    wides = (base_ref, crossed_ref, mix_ref)
    for a in range(3):
        order = row_order(a, me)
        mine[a] = contract_last(order[0:256], factors[a][...]).astype(jnp.bfloat16)
        theirs[a] = contract_last(order[256:512], factors[a][...]).astype(jnp.bfloat16)

    pl.semaphore_wait(barrier, 127)
    partner = (y * 4 + z, x * 2 + 1 - core)
    pair = []
    for a in range(3):
        for i, (src, dst) in enumerate(((theirs.at[a], lefts.at[a]), (wides[a], rights.at[a]))):
            copy = pltpu.make_async_remote_copy(
                src_ref=src,
                dst_ref=dst,
                send_sem=pair_send.at[a, i],
                recv_sem=pair_recv.at[a, i],
                device_id=partner,
                device_id_type=MESH,
            )
            copy.start()
            pair.append(copy)

    def slots(m, _):
        at = pl.multiple_of(m * 256, 256)
        slot = lax.broadcasted_iota(jnp.int32, (256, 256), 0) + at
        picks = jnp.concatenate(
            [hot(slot == (slots_ref[t : t + 1, :] & 1023)) for t in range(26)], axis=1
        )
        sums = jnp.dot(picks, split[...], preferred_element_type=jnp.float32)
        for side in range(2):
            for block in range(2):
                i = side * 8 + m * 2 + block
                here = pl.ds(pl.multiple_of(i * 128, 128), 128)
                total = sums[128 * block : 128 * block + 128, 128 * side : 128 * side + 128]
                gone = to_column(evict_ref[pl.ds(i, 1), :].astype(jnp.float32))
                cache_ref[here, :] = total * (1.0 - gone)
                sent = total * gone
                upper = to_column(pos_ref[pl.ds(i, 1), :]) >> 11
                placed[here, 0:128] = jnp.where(upper == 0, sent, 0.0).astype(jnp.bfloat16)
                placed[here, 128:256] = jnp.where(upper == 1, sent, 0.0).astype(jnp.bfloat16)
        return 0

    lax.fori_loop(0, 4, slots, 0)

    def send(j, _):
        at = pl.multiple_of(j * 256, 256)
        place = lax.broadcasted_iota(jnp.int32, (256, 128), 0) + at
        picks = jnp.concatenate(
            [hot(place == (pos_ref[i : i + 1, :] & 2047)) for i in range(16)], axis=1
        )
        sums = jnp.dot(picks, placed[...], preferred_element_type=jnp.float32)
        for side in range(2):
            d = j + 8 * side
            start = pl.multiple_of(d * 256, 256)
            out[pl.ds(start, 256), :] = sums[:, 128 * side : 128 * side + 128].astype(jnp.bfloat16)
            host = ((y + d // 4) % 4) * 4 + (z + d % 4) % 4
            back = ((4 - d // 4) % 4) * 4 + (4 - d % 4) % 4
            for e in range(8):

                def go():
                    pltpu.make_async_remote_copy(
                        src_ref=out.at[pl.ds(pl.multiple_of(start + 32 * e, 32), 32), :],
                        dst_ref=rcv.at[
                            pl.ds(pl.multiple_of(back * 256 + 32 * neg_chip(e), 32), 32), :
                        ],
                        send_sem=grad_send,
                        recv_sem=grad_recv,
                        device_id=(host, chips[e]),
                        device_id_type=MESH,
                    ).start()

                if e == 0 and side == 0:
                    pl.when(d > 0)(go)
                else:
                    go()
        return 0

    lax.fori_loop(0, 8, send, 0)
    rcv[0:32, :] = out[0:32, :]

    def hop(a, stage, step, src, dst):
        copy = pltpu.make_async_remote_copy(
            src_ref=src,
            dst_ref=dst,
            send_sem=sum_send.at[a, stage, step - 1],
            recv_sem=sum_recv.at[a, stage, step - 1],
            device_id=shifted(me, AXES[a][stage], step),
            device_id_type=MESH,
        )
        copy.start()
        return copy

    hops = []
    for a in range(3):
        pair[2 * a].wait_recv()
        pair[2 * a + 1].wait_recv()

        def product(j, _):
            cols = pl.ds(pl.multiple_of(j * 512, 512), 512)
            sums = jnp.dot(mine[a], wides[a][:, cols], preferred_element_type=jnp.float32)
            sums = sums + jnp.dot(lefts[a], rights[a, :, cols], preferred_element_type=jnp.float32)
            part[a, :, cols] = sums.astype(jnp.bfloat16)
            return 0

        lax.fori_loop(0, 7, product, 0)
        hops.append(
            [
                hop(a, 0, step, part.at[a, pl.ds(64 * step, 64), :], first.at[a, step - 1])
                for step in (2, 1, 3)
            ]
        )

    whole = pl.ds(32, 4064)
    pltpu.make_async_copy(rcv.at[whole, :], rcv.at[whole, :], grad_recv).wait()
    inc = inc_ref[...]
    inc_t = inc.T
    for k in range(128):
        g, c = k % 32, k // 32
        half = jnp.broadcast_to(inc_t[0:32, k : k + 1] >> 11, (32, 128))
        grad = rcv[32 * k : 32 * k + 32, :].astype(jnp.float32)
        at = (g * 4 + c) * 32
        spread[at : at + 32, 0:128] = jnp.where(half == 0, grad, 0.0).astype(jnp.bfloat16)
        spread[at : at + 32, 128:256] = jnp.where(half == 1, grad, 0.0).astype(jnp.bfloat16)
    asked = jnp.concatenate([inc[32 * c : 32 * c + 32, 0:32] for c in range(4)], axis=1) & 2047

    def update(m, _):
        at = pl.multiple_of(m * 256, 256)
        row = lax.broadcasted_iota(jnp.int32, (256, 128), 0) + at
        picks = jnp.concatenate([hot(row == asked[g : g + 1, :]) for g in range(32)], axis=1)
        sums = jnp.dot(picks, spread[...], preferred_element_type=jnp.float32)
        for side in range(2):
            for block in range(2):
                i = side * 16 + m * 2 + block
                here = pl.ds(pl.multiple_of(i * 128, 128), 128)
                row_grad = sums[128 * block : 128 * block + 128, 128 * side : 128 * side + 128]
                acc = to_column(acc_ref[pl.ds(i, 1), :])
                acc = acc + jnp.sum(row_grad * row_grad, axis=1, keepdims=True) * (1.0 / 128.0)
                new_acc_ref[pl.ds(i, 1), :] = acc.T[0:1, :]
                values = rows_ref[here, :].astype(jnp.float32) * to_column(scale_ref[pl.ds(i, 1), :])
                values = values - LEARN_RATE * row_grad / jnp.sqrt(acc)
                top = jnp.max(jnp.abs(values), axis=1, keepdims=True)
                scale = (jnp.broadcast_to(top, (128, 128)) + 1e-06) / QUANT_TOP
                new_scale_ref[pl.ds(i, 1), :] = scale.T[0:1, :]
                new_rows_ref[here, :] = (values / scale).astype(jnp.bfloat16)
        return 0

    lax.fori_loop(0, 8, update, 0)

    for a in range(3):
        for copy in hops[a]:
            copy.wait_recv()

        def gather(j, _):
            cols = pl.ds(pl.multiple_of(j * 512, 512), 512)
            sums = part[a, 0:64, cols].astype(jnp.float32)
            for step in range(3):
                sums = sums + first[a, step, :, cols].astype(jnp.float32)
            second_src[a, :, cols] = sums.astype(jnp.bfloat16)
            return 0

        lax.fori_loop(0, 7, gather, 0)
        hops[a] = hops[a] + [
            hop(a, 1, step, second_src.at[a, pl.ds(16 * step, 16), :], second.at[a, step - 1])
            for step in (2, 1, 3)
        ]
    for a in range(3):
        for copy in hops[a][3:]:
            copy.wait_recv()
        sums = second_src[a, 0:16, :].astype(jnp.float32)
        for step in range(3):
            sums = sums + second[a, step].astype(jnp.float32)
        for step in range(4):
            piece = sums[4 * step : 4 * step + 4, :]
            third_src[a, step] = jnp.concatenate(
                [piece[:, 896 * i : 896 * i + 896] for i in range(4)], axis=0
            ).astype(jnp.bfloat16)
        hops[a] = hops[a] + [
            hop(a, 2, step, third_src.at[a, step], third.at[a, step - 1]) for step in (2, 1, 3)
        ]
    for a, out_ref in enumerate((out_down_ref, out_hid_ref, out_up_ref)):
        for copy in hops[a][6:]:
            copy.wait_recv()
        sums = third_src[a, 0].astype(jnp.float32)
        for step in range(3):
            sums = sums + third[a, step].astype(jnp.float32)
        sums = sums * (1.0 / 128.0)
        sums = jnp.concatenate([sums[4 * i : 4 * i + 4, :] for i in range(4)], axis=1)
        out_ref[...] = sums[:, 0:3341]

    for copy in pair + hops[0] + hops[1] + hops[2]:
        copy.wait_send()
    pltpu.make_async_copy(out.at[whole, :], out.at[whole, :], grad_send).wait()


def update(*operands):
    vmem = pl.BlockSpec(memory_space=pltpu.VMEM)
    bf16, f32 = jnp.bfloat16, jnp.float32
    dense_out = jax.ShapeDtypeStruct((4, 3341), f32)
    return pl.pallas_call(
        update_kernel,
        name="update",
        out_shape=(
            jax.ShapeDtypeStruct((4096, 128), bf16),
            jax.ShapeDtypeStruct((32, 128), f32),
            jax.ShapeDtypeStruct((32, 128), f32),
            jax.ShapeDtypeStruct((2048, 128), f32),
            dense_out,
            dense_out,
            dense_out,
        ),
        in_specs=[vmem] * 14,
        out_specs=(vmem,) * 7,
        scratch_shapes=[
            pltpu.VMEM((6656, 256), bf16),
            pltpu.VMEM((2048, 256), bf16),
            pltpu.VMEM((4096, 128), bf16),
            pltpu.VMEM((4096, 128), bf16),
            pltpu.VMEM((4096, 256), bf16),
            pltpu.VMEM((3, 256, 256), bf16),
            pltpu.VMEM((3, 256, 256), bf16),
            pltpu.VMEM((3, 256, 256), bf16),
            pltpu.VMEM((3, 256, 3584), bf16),
            pltpu.VMEM((3, 256, 3584), bf16),
            pltpu.VMEM((3, 3, 64, 3584), bf16),
            pltpu.VMEM((3, 64, 3584), bf16),
            pltpu.VMEM((3, 3, 16, 3584), bf16),
            pltpu.VMEM((3, 4, 16, 896), bf16),
            pltpu.VMEM((3, 3, 16, 896), bf16),
            pltpu.SemaphoreType.DMA((3, 2)),
            pltpu.SemaphoreType.DMA((3, 2)),
            pltpu.SemaphoreType.DMA,
            pltpu.SemaphoreType.DMA,
            pltpu.SemaphoreType.DMA((3, 3, 3)),
            pltpu.SemaphoreType.DMA((3, 3, 3)),
        ],
        compiler_params=pltpu.CompilerParams(
            collective_id=1, has_side_effects=True, vmem_limit_bytes=56 * 2**20
        ),
    )(*operands)


def on_device(
    dense_feats,
    labels,
    slot_ids,
    needed_owner,
    needed_local,
    evicted,
    table_rows,
    table_scale,
    table_acc,
    cross_down,
    cross_up,
    cross_bias,
    hidden_weight,
    hidden_bias,
    out_weight,
):
    slots_t = slot_ids.T
    up_t = cross_up.T
    scale = table_scale.reshape(32, 128)
    base, pos, asked = embed(
        needed_owner.reshape(1, 2048),
        needed_local.reshape(1, 2048),
        slots_t,
        table_rows,
        scale,
        jnp.pad(dense_feats, ((0, 0), (0, 243))),
    )
    tails = jnp.concatenate([cross_down[3328:], up_t[3328:], hidden_weight[3328:]], axis=1)
    grad, crossed, mix, low, grad_hid, grad_low = dense(
        base,
        labels.astype(jnp.float32).reshape(1, 256),
        cross_down,
        up_t,
        hidden_weight,
        jnp.pad(tails, ((0, 243), (0, 0))),
        jnp.pad(cross_bias, (0, 243)).reshape(1, 3584),
        hidden_bias.reshape(1, 512),
        out_weight.astype(jnp.float32).reshape(1, 512),
    )
    new_rows, new_scale, new_acc, cache, grad_down, grad_hidden, grad_up = update(
        grad,
        base,
        crossed,
        mix,
        low,
        grad_hid,
        grad_low,
        pos.reshape(16, 128),
        asked,
        slots_t,
        evicted.reshape(16, 128),
        table_rows,
        scale,
        table_acc.reshape(32, 128),
    )
    return (
        new_rows,
        new_scale.reshape(4096),
        new_acc.reshape(4096),
        cache,
        grad_down,
        grad_hidden,
        grad_up,
    )


def solution(mesh):
    placed = (
        P(("hst", "chip"), None),
        P(("hst", "chip")),
        P(("hst", "chip"), None),
        P(("hst", "chip"), None),
        P(("hst", "chip")),
        P(("hst", "chip")),
        P(("hst", "chip"), None),
        P(("hst", "chip")),
        P(("hst", "chip")),
        P(),
        P(),
        P(),
        P(),
        P(),
        P(),
    )
    return jax.shard_map(
        on_device,
        mesh=mesh,
        in_specs=placed,
        out_specs=(
            P(("hst", "chip"), None),
            P(("hst", "chip")),
            P(("hst", "chip")),
            P(("hst", "chip"), None),
            P(("hst", "chip"), None),
            P(("hst", "chip"), None),
            P(("hst", "chip"), None),
        ),
        check_vma=False,
    )
```

```python
import functools

import jax
import jax.experimental.pallas as pl
import jax.experimental.pallas.tpu as pltpu
import jax.numpy as jnp
from jax import lax
from jax.sharding import PartitionSpec as P

MESH = pl.DeviceIdType.MESH
LEARN_RATE = 0.1
QUANT_TOP = 4.0


def contract_last(left, right):
    return lax.dot_general(
        left, right, (((1,), (1,)), ((), ())), preferred_element_type=jnp.float32
    )


def contract_first(left, right):
    return lax.dot_general(
        left, right, (((0,), (0,)), ((), ())), preferred_element_type=jnp.float32
    )


def coords():
    host = lax.axis_index("hst")
    chip = lax.axis_index("chip")
    return host // 4, host % 4, chip // 2, chip % 2


def hosts_from(y, z):
    return [((y + d // 4) % 4) * 4 + (z + d % 4) % 4 for d in range(16)]


def chips_from(x, core):
    return [((x + d // 2) % 4) * 2 + (core + d % 2) % 2 for d in range(8)]


def neg_host(d):
    return ((4 - d // 4) % 4) * 4 + (4 - d % 4) % 4


def neg_chip(d):
    return ((4 - d // 2) % 4) * 2 + d % 2


def greet_all(barrier):
    y, z, x, core = coords()
    chips = chips_from(x, core)

    def one(d, _):
        host = ((y + d // 4) % 4) * 4 + (z + d % 4) % 4
        for e in range(8):
            if e == 0:

                @pl.when(d > 0)
                def _():
                    pl.semaphore_signal(barrier, inc=1, device_id=(host, chips[0]), device_id_type=MESH)

            else:
                pl.semaphore_signal(barrier, inc=1, device_id=(host, chips[e]), device_id_type=MESH)
        return 0

    lax.fori_loop(0, 16, one, 0)


def hot(cond):
    return jnp.where(cond, 1.0, 0.0).astype(jnp.bfloat16)


def to_column(row):
    return jnp.broadcast_to(row, (128, 128)).T


def lane_tiles(col, count):
    lane = lax.broadcasted_iota(jnp.int32, col.shape, 1)
    return jnp.concatenate([hot(col == lane + 128 * i) for i in range(count)], axis=1)


AXES = (("y", "z", "x"), ("z", "x", "y"), ("x", "y", "z"))
DOWN, UP, HID = 0, 1, 2


def row_order(array, me):
    row = lax.broadcasted_iota(jnp.int32, (512, 512), 0)
    at = {"core": (me["core"] + (row >> 8)) & 1}
    for stage, axis in enumerate(AXES[array]):
        at[axis] = (me[axis] + (row >> (6 - 2 * stage))) & 3
    source = (at["y"] * 32 + at["z"] * 8 + at["x"] * 2 + at["core"]) * 4 + (row & 3)
    return hot(source == lax.broadcasted_iota(jnp.int32, (512, 512), 1))


def shifted(me, axis, step):
    to = dict(me)
    to[axis] = (me[axis] + step) % 4
    return (to["y"] * 4 + to["z"], to["x"] * 2 + to["core"])


def step_kernel(
    owner_ref,
    local_ref,
    slots_ref,
    feats_ref,
    labels_ref,
    evict_ref,
    rows_hbm,
    scale_ref,
    acc_ref,
    down_hbm,
    up_hbm,
    hid_hbm,
    down_tail,
    up_tail,
    hid_tail,
    bias_ref,
    hid_bias_ref,
    out_w_ref,
    new_rows_hbm,
    new_scale_ref,
    new_acc_ref,
    cache_hbm,
    out_down_ref,
    out_hid_ref,
    out_up_ref,
    rows_ref,
    new_rows_ref,
    cache_ref,
    weights,
    bias,
    req,
    inc,
    asked_ref,
    val,
    ret,
    rcv,
    table2,
    qcol,
    pos,
    poscol,
    fetched,
    fetched2,
    factor,
    wides,
    rights,
    low_ref,
    grad_hid_ref,
    grad_low_ref,
    split,
    placed,
    spread,
    mine,
    theirs,
    lefts,
    first,
    second_src,
    second,
    third_src,
    third,
    load_sems,
    side_sems,
    req_send,
    req_recv,
    val_send,
    val_recv,
    pair_send,
    pair_recv,
    grad_send,
    grad_recv,
    sum_send,
    sum_recv,
):
    y, z, x, core = coords()
    me = {"y": y, "z": z, "x": x, "core": core}
    chips = chips_from(x, core)
    partner = (y * 4 + z, x * 2 + 1 - core)
    barrier = pltpu.get_barrier_semaphore()
    greet_all(barrier)
    base, crossed, mix = wides.at[0], wides.at[1], wides.at[2]

    rows_load = pltpu.make_async_copy(rows_hbm, rows_ref, side_sems.at[0])
    rows_load.start()
    loads = []
    for i, src in enumerate((down_hbm, up_hbm, hid_hbm)):
        some = []
        for j in range(13):
            copy = pltpu.make_async_copy(
                src.at[pl.ds(256 * j, 256), :], weights.at[i, j], load_sems.at[i, j]
            )
            copy.start()
            some.append(copy)
        loads.append(some)

    owner = owner_ref[...]
    rel = (
        (((owner >> 5) - y) & 3) * 32
        + (((owner >> 3) - z) & 3) * 8
        + (((owner >> 1) - x) & 3) * 2
        + ((owner - core) & 1)
    )
    sub = lax.broadcasted_iota(jnp.int32, (128, 256), 0)
    upper = hot(
        lax.broadcasted_iota(jnp.int32, (256, 256), 0)
        < lax.broadcasted_iota(jnp.int32, (256, 256), 1)
    )
    seen = jnp.zeros((128, 1), jnp.float32)
    hi_sum = jnp.zeros((128, 32), jnp.float32)
    lo_sum = jnp.zeros((128, 32), jnp.float32)
    for i in range(8):
        part = rel[:, 256 * i : 256 * i + 256]
        hits = hot(part == sub)
        before = jnp.dot(hits, upper, preferred_element_type=jnp.float32) + seen
        wide = hits.astype(jnp.float32)
        place = jnp.sum(wide * before, axis=0, keepdims=True).astype(jnp.int32)
        seen = seen + jnp.sum(wide, axis=1, keepdims=True)
        where = part * 32 + place
        pos[2 * i : 2 * i + 1, :] = where[:, 0:128]
        pos[2 * i + 1 : 2 * i + 2, :] = where[:, 128:256]
        code = local_ref[:, 256 * i : 256 * i + 256] + 1
        here = place == lax.broadcasted_iota(jnp.int32, (32, 256), 0)
        hi = jnp.where(here, (code >> 6).astype(jnp.float32), 0.0).astype(jnp.bfloat16)
        lo = jnp.where(here, (code & 63).astype(jnp.float32), 0.0).astype(jnp.bfloat16)
        hi_sum = hi_sum + contract_last(hits, hi)
        lo_sum = lo_sum + contract_last(hits, lo)
    asked = (hi_sum * 64.0 + lo_sum).astype(jnp.int32) - 1
    asked = jnp.concatenate([asked, jnp.full((128, 96), -1, jnp.int32)], axis=1)
    for k in range(128):
        req[k] = asked[k : k + 1, :]
    inc[0] = req[0]

    pl.semaphore_wait(barrier, 127)

    def ask(d, _):
        host = ((y + d // 4) % 4) * 4 + (z + d % 4) % 4
        back = ((4 - d // 4) % 4) * 4 + (4 - d % 4) % 4
        for e in range(8):

            def go():
                pltpu.make_async_remote_copy(
                    src_ref=req.at[d * 8 + e],
                    dst_ref=inc.at[back * 8 + neg_chip(e)],
                    send_sem=req_send,
                    recv_sem=req_recv,
                    device_id=(host, chips[e]),
                    device_id_type=MESH,
                ).start()

            if e == 0:
                pl.when(d > 0)(go)
            else:
                go()
        return 0

    lax.fori_loop(0, 16, ask, 0)

    rows_load.wait()
    for i in range(32):
        rows = rows_ref[128 * i : 128 * i + 128, :].astype(jnp.float32)
        col = to_column(scale_ref[i : i + 1, :])
        table2[
            (i % 8) * 128 : (i % 8) * 128 + 128, (i // 8) * 128 : (i // 8) * 128 + 128
        ] = (rows * col).astype(jnp.bfloat16)
    for i in range(16):
        poscol[128 * i : 128 * i + 128, :] = to_column(pos[i : i + 1, :])
    ids = jnp.concatenate([slots_ref[...], jnp.zeros((102, 256), jnp.int32)], axis=0).T
    ids = ids.astype(jnp.float32)
    for t in range(26):
        factor[t] = jnp.broadcast_to(ids[:, t : t + 1], (256, 128))
    feats = jnp.concatenate(
        [feats_ref[...].astype(jnp.float32), jnp.zeros((115, 256), jnp.float32)], axis=0
    )
    base[:, 3328:3456] = feats.T.astype(jnp.bfloat16)
    base[:, 3456:3584] = jnp.zeros((256, 128), jnp.bfloat16)
    bias[...] = jnp.zeros((1, 3584), jnp.float32)
    bias[:, 0:3341] = bias_ref[...].reshape(1, 3341)
    inside = lax.broadcasted_iota(jnp.int32, (128, 512), 0) < 13
    for i, tail in enumerate((down_tail, up_tail, hid_tail)):
        weights[i, 13, 0:128, :] = jnp.where(inside, tail[...].astype(jnp.float32), 0.0).astype(
            jnp.bfloat16
        )
        weights[i, 13, 128:256, :] = jnp.zeros((128, 512), jnp.bfloat16)

    pltpu.make_async_copy(req.at[pl.ds(0, 127)], req.at[pl.ds(0, 127)], req_send).wait()
    pltpu.make_async_copy(inc.at[pl.ds(1, 127)], inc.at[pl.ds(1, 127)], req_recv).wait()
    got = inc[...].reshape(128, 128)
    asked_ref[...] = got
    got_t = got.T
    for k in range(128):
        qcol[32 * k : 32 * k + 32, :] = jnp.broadcast_to(got_t[0:32, k : k + 1], (32, 128))

    def send_blocks(d, skip_self, src, dst, send_sem, recv_sem):
        start = pl.multiple_of(d * 256, 256)
        host = ((y + d // 4) % 4) * 4 + (z + d % 4) % 4
        back = ((4 - d // 4) % 4) * 4 + (4 - d % 4) % 4
        for e in range(8):

            def go():
                pltpu.make_async_remote_copy(
                    src_ref=src.at[pl.ds(pl.multiple_of(start + 32 * e, 32), 32), :],
                    dst_ref=dst.at[pl.ds(pl.multiple_of(back * 256 + 32 * neg_chip(e), 32), 32), :],
                    send_sem=send_sem,
                    recv_sem=recv_sem(back // 4),
                    device_id=(host, chips[e]),
                    device_id_type=MESH,
                ).start()

            if e == 0 and skip_self:
                pl.when(d > 0)(go)
            else:
                go()

    def serve(i, _):
        at = pl.multiple_of(i * 512, 512)
        query = qcol[pl.ds(at, 512), :]
        found = jnp.dot(
            lane_tiles(query & 1023, 8), table2[...], preferred_element_type=jnp.float32
        )
        quarter = query >> 10
        result = jnp.zeros((512, 128), jnp.float32)
        for q in range(4):
            result = jnp.where(quarter == q, found[:, 128 * q : 128 * q + 128], result)
        val[pl.ds(at, 512), :] = result.astype(jnp.bfloat16)
        send_blocks(2 * i, True, val, ret, val_send, lambda c: val_recv.at[c])
        send_blocks(2 * i + 1, False, val, ret, val_send, lambda c: val_recv.at[c])
        return 0

    lax.fori_loop(0, 8, serve, 0)
    ret[0:32, :] = val[0:32, :]
    for chunk in (0, 3, 2, 1):
        if chunk == 0:
            landed = ret.at[pl.ds(32, 992), :]
        else:
            landed = ret.at[pl.ds(1024 * chunk, 1024), :]
        pltpu.make_async_copy(landed, landed, val_recv.at[chunk]).wait()
        sides = jnp.concatenate(
            [
                ret[1024 * chunk : 1024 * chunk + 512, :],
                ret[1024 * chunk + 512 : 1024 * chunk + 1024, :],
            ],
            axis=1,
        )

        def pick(i, _):
            at = pl.multiple_of(i * 512, 512)
            where = poscol[pl.ds(at, 512), :]
            found = jnp.dot(lane_tiles(where & 511, 4), sides, preferred_element_type=jnp.float32)
            half = where >> 9
            if chunk == 0:
                result = jnp.zeros((512, 128), jnp.float32)
            else:
                result = fetched[pl.ds(at, 512), :]
            result = jnp.where(half == 2 * chunk, found[:, :128], result)
            fetched[pl.ds(at, 512), :] = jnp.where(half == 2 * chunk + 1, found[:, 128:], result)
            return 0

        lax.fori_loop(0, 4, pick, 0)
    fetched2[:, 0:128] = fetched[0:1024, :].astype(jnp.bfloat16)
    fetched2[:, 128:256] = fetched[1024:2048, :].astype(jnp.bfloat16)

    def fill(i, _):
        slot = factor[pl.ds(2 * i, 2)].reshape(512, 128).astype(jnp.int32)
        found = jnp.dot(
            lane_tiles(slot & 1023, 8), fetched2[...], preferred_element_type=jnp.float32
        )
        result = jnp.where(slot < 1024, found[:, :128], found[:, 128:]).astype(jnp.bfloat16)
        base[:, pl.ds(pl.multiple_of(256 * i, 128), 128)] = result[0:256]
        base[:, pl.ds(pl.multiple_of(256 * i + 128, 128), 128)] = result[256:512]
        return 0

    lax.fori_loop(0, 13, fill, 0)

    def give(array, side, src, dst):
        copy = pltpu.make_async_remote_copy(
            src_ref=src,
            dst_ref=dst,
            send_sem=pair_send.at[array, side],
            recv_sem=pair_recv.at[array, side],
            device_id=partner,
            device_id_type=MESH,
        )
        copy.start()
        return copy

    def ordered(array, values):
        order = row_order(array, me)
        mine[array] = contract_last(order[0:256], values).astype(jnp.bfloat16)
        theirs[array] = contract_last(order[256:512], values).astype(jnp.bfloat16)
        return give(array, 0, theirs.at[array], lefts.at[array])

    pair = [give(0, 1, base, rights.at[0])]
    for copy in loads[DOWN]:
        copy.wait()
    low = jnp.dot(
        base[...], weights[DOWN].reshape(3584, 512), preferred_element_type=jnp.float32
    ).astype(jnp.bfloat16)
    low_ref[...] = low
    for copy in loads[UP]:
        copy.wait()

    def cross(j, _):
        cols = pl.ds(pl.multiple_of(j * 256, 256), 256)
        mixing = contract_last(low_ref[...], weights[UP, j]) + bias[:, cols]
        wide = base[:, cols].astype(jnp.float32)
        crossed[:, cols] = (wide * mixing + wide).astype(jnp.bfloat16)
        factor[2 * j] = mixing[:, 0:128] + 1.0
        factor[2 * j + 1] = mixing[:, 128:256] + 1.0
        return 0

    lax.fori_loop(0, 14, cross, 0)
    pair.append(give(1, 1, crossed, rights.at[1]))
    pair.append(ordered(2, low_ref[...]))
    for copy in loads[HID]:
        copy.wait()
    preact = (
        jnp.dot(
            crossed[...], weights[HID].reshape(3584, 512), preferred_element_type=jnp.float32
        )
        + hid_bias_ref[...]
    )
    sig = jax.nn.sigmoid(preact)
    hidden = (preact * sig).astype(jnp.bfloat16).astype(jnp.float32)
    out_w = out_w_ref[...].astype(jnp.float32).reshape(1, 512)
    logits = jnp.sum(hidden * out_w, axis=1, keepdims=True)
    labels = labels_ref[...].astype(jnp.float32)
    labels = jnp.concatenate([to_column(labels[:, 0:128]), to_column(labels[:, 128:256])], axis=0)
    grad_logit = jax.nn.sigmoid(logits) - labels[:, 0:1]
    grad_hid_ref[...] = (grad_logit * out_w * (sig * (1.0 + preact * (1.0 - sig)))).astype(
        jnp.bfloat16
    )
    pair.append(ordered(1, grad_hid_ref[...]))

    def back(j, _):
        cols = pl.ds(pl.multiple_of(j * 256, 256), 256)
        grad_cross = contract_last(grad_hid_ref[...], weights[HID, j])
        mix[:, cols] = (grad_cross * base[:, cols].astype(jnp.float32)).astype(jnp.bfloat16)
        factor[2 * j] = grad_cross[:, 0:128] * factor[2 * j]
        factor[2 * j + 1] = grad_cross[:, 128:256] * factor[2 * j + 1]
        return 0

    lax.fori_loop(0, 14, back, 0)
    pair.append(give(2, 1, mix, rights.at[2]))
    grad_low_ref[...] = jnp.dot(
        mix[...], weights[UP].reshape(3584, 512), preferred_element_type=jnp.float32
    ).astype(jnp.bfloat16)
    pair.append(ordered(0, grad_low_ref[...]))

    room = ((UP, 0), (HID, 0), (HID, 7))

    def hop(a, stage, step, src, dst):
        copy = pltpu.make_async_remote_copy(
            src_ref=src,
            dst_ref=dst,
            send_sem=sum_send.at[a, stage, step - 1],
            recv_sem=sum_recv.at[a, stage, step - 1],
            device_id=shifted(me, AXES[a][stage], step),
            device_id_type=MESH,
        )
        copy.start()
        return copy

    hops = [[], [], []]

    def multiply(a):
        place, at = room[a]

        def product(j, _):
            cols = pl.ds(pl.multiple_of(j * 512, 512), 512)
            both = jnp.concatenate([mine[a], lefts[a]], axis=1)
            wide = jnp.concatenate([wides[a, :, cols], rights[a, :, cols]], axis=0)
            weights[place, at + j] = jnp.dot(both, wide, preferred_element_type=jnp.float32).astype(
                jnp.bfloat16
            )
            return 0

        lax.fori_loop(0, 7, product, 0)
        for step in (2, 1, 3):
            src = weights.at[place, pl.ds(at, 7), pl.ds(64 * step, 64), :]
            hops[a].append(hop(a, 0, step, src, first.at[a, step - 1]))

    pair[1].wait_recv()
    pair[3].wait_recv()
    multiply(1)
    pair[2].wait_recv()
    pair[4].wait_recv()
    multiply(2)

    def last(j, _):
        grad = contract_last(grad_low_ref[...], weights[DOWN, j])
        for side in range(2):
            t = 2 * j + side
            wide = grad[:, 128 * side : 128 * side + 128] + factor[t]
            here = pl.ds(pl.multiple_of(t * 256, 256), 256)
            split[here, :] = jnp.concatenate([wide, wide], axis=1).astype(jnp.bfloat16)
        return 0

    lax.fori_loop(0, 13, last, 0)
    pair[0].wait_recv()
    pair[5].wait_recv()
    multiply(0)
    ids = jnp.concatenate([slots_ref[...], jnp.zeros((102, 256), jnp.int32)], axis=0).T
    for t in range(26):
        half = jnp.broadcast_to(ids[:, t : t + 1] >> 10, (256, 128))
        low_side = split[256 * t : 256 * t + 256, 0:128].astype(jnp.float32)
        split[256 * t : 256 * t + 256, 0:128] = jnp.where(half == 0, low_side, 0.0).astype(
            jnp.bfloat16
        )
        split[256 * t : 256 * t + 256, 128:256] = jnp.where(half == 1, low_side, 0.0).astype(
            jnp.bfloat16
        )

    def slots(m, _):
        at = pl.multiple_of(m * 256, 256)
        slot = lax.broadcasted_iota(jnp.int32, (256, 256), 0) + at
        picks = jnp.concatenate(
            [hot(slot == (slots_ref[t : t + 1, :] & 1023)) for t in range(26)], axis=1
        )
        sums = jnp.dot(picks, split[...], preferred_element_type=jnp.float32)
        for side in range(2):
            for block in range(2):
                i = side * 8 + m * 2 + block
                here = pl.ds(pl.multiple_of(i * 128, 128), 128)
                total = sums[128 * block : 128 * block + 128, 128 * side : 128 * side + 128]
                gone = to_column(evict_ref[pl.ds(i, 1), :].astype(jnp.float32))
                cache_ref[here, :] = total * (1.0 - gone)
                sent = total * gone
                upper = poscol[here, :] >> 11
                placed[here, 0:128] = jnp.where(upper == 0, sent, 0.0).astype(jnp.bfloat16)
                placed[here, 128:256] = jnp.where(upper == 1, sent, 0.0).astype(jnp.bfloat16)
        return 0

    lax.fori_loop(0, 4, slots, 0)
    cache_out = pltpu.make_async_copy(cache_ref, cache_hbm, side_sems.at[1])
    cache_out.start()
    whole = pl.ds(32, 4064)
    pltpu.make_async_copy(val.at[whole, :], val.at[whole, :], val_send).wait()

    def send(j, _):
        at = pl.multiple_of(j * 512, 512)
        place = lax.broadcasted_iota(jnp.int32, (512, 128), 0) + at
        picks = jnp.concatenate(
            [hot(place == (pos[i : i + 1, :] & 2047)) for i in range(16)], axis=1
        )
        sums = jnp.dot(picks, placed[...], preferred_element_type=jnp.float32)
        for side in range(2):
            val[pl.ds(pl.multiple_of(at + 2048 * side, 512), 512), :] = sums[
                :, 128 * side : 128 * side + 128
            ].astype(jnp.bfloat16)
            for more in range(2):
                send_blocks(
                    2 * j + more + 8 * side,
                    side == 0 and more == 0,
                    val,
                    rcv,
                    grad_send,
                    lambda c: grad_recv,
                )
        return 0

    lax.fori_loop(0, 4, send, 0)
    rcv[0:32, :] = val[0:32, :]

    for a in (1, 2, 0):
        place, at = room[a]
        for copy in hops[a]:
            copy.wait_recv()

        def gather(j, _):
            sums = weights[place, at + j, 0:64, :].astype(jnp.float32)
            for step in range(3):
                sums = sums + first[a, step, j].astype(jnp.float32)
            second_src[a, :, pl.ds(pl.multiple_of(j * 512, 512), 512)] = sums.astype(jnp.bfloat16)
            return 0

        lax.fori_loop(0, 7, gather, 0)
        for step in (2, 1, 3):
            src = second_src.at[a, pl.ds(16 * step, 16), :]
            hops[a].append(hop(a, 1, step, src, second.at[a, step - 1]))

    pltpu.make_async_copy(rcv.at[whole, :], rcv.at[whole, :], grad_recv).wait()
    for k in range(128):
        g, c = k % 32, k // 32
        half = qcol[32 * k : 32 * k + 32, :] >> 11
        grad = rcv[32 * k : 32 * k + 32, :].astype(jnp.float32)
        at = (g * 4 + c) * 32
        spread[at : at + 32, 0:128] = jnp.where(half == 0, grad, 0.0).astype(jnp.bfloat16)
        spread[at : at + 32, 128:256] = jnp.where(half == 1, grad, 0.0).astype(jnp.bfloat16)
    asked = asked_ref[...]
    asked = jnp.concatenate([asked[32 * c : 32 * c + 32, 0:32] for c in range(4)], axis=1) & 2047

    def update(m, _):
        at = pl.multiple_of(m * 256, 256)
        row = lax.broadcasted_iota(jnp.int32, (256, 128), 0) + at
        picks = jnp.concatenate([hot(row == asked[g : g + 1, :]) for g in range(32)], axis=1)
        sums = jnp.dot(picks, spread[...], preferred_element_type=jnp.float32)
        for side in range(2):
            for block in range(2):
                i = side * 16 + m * 2 + block
                here = pl.ds(pl.multiple_of(i * 128, 128), 128)
                row_grad = sums[128 * block : 128 * block + 128, 128 * side : 128 * side + 128]
                acc = to_column(acc_ref[pl.ds(i, 1), :])
                acc = acc + jnp.sum(row_grad * row_grad, axis=1, keepdims=True) * (1.0 / 128.0)
                new_acc_ref[pl.ds(i, 1), :] = acc.T[0:1, :]
                values = rows_ref[here, :].astype(jnp.float32) * to_column(scale_ref[pl.ds(i, 1), :])
                values = values - LEARN_RATE * row_grad / jnp.sqrt(acc)
                top = jnp.max(jnp.abs(values), axis=1, keepdims=True)
                scale = (jnp.broadcast_to(top, (128, 128)) + 1e-06) / QUANT_TOP
                new_scale_ref[pl.ds(i, 1), :] = scale.T[0:1, :]
                new_rows_ref[here, :] = (values / scale).astype(jnp.bfloat16)
        return 0

    lax.fori_loop(0, 4, update, 0)

    for a in (1, 2, 0):
        for copy in hops[a][3:]:
            copy.wait_recv()
        sums = second_src[a, 0:16, :].astype(jnp.float32)
        for step in range(3):
            sums = sums + second[a, step].astype(jnp.float32)
        for step in range(4):
            piece = sums[4 * step : 4 * step + 4, :]
            third_src[a, step] = jnp.concatenate(
                [piece[:, 896 * i : 896 * i + 896] for i in range(4)], axis=0
            ).astype(jnp.bfloat16)
        for step in (2, 1, 3):
            hops[a].append(hop(a, 2, step, third_src.at[a, step], third.at[a, step - 1]))

    lax.fori_loop(4, 8, update, 0)
    rows_out = pltpu.make_async_copy(new_rows_ref, new_rows_hbm, side_sems.at[2])
    rows_out.start()

    for a, out_ref in enumerate((out_down_ref, out_hid_ref, out_up_ref)):
        for copy in hops[a][6:]:
            copy.wait_recv()
        sums = third_src[a, 0].astype(jnp.float32)
        for step in range(3):
            sums = sums + third[a, step].astype(jnp.float32)
        sums = sums * (1.0 / 128.0)
        sums = jnp.concatenate([sums[4 * i : 4 * i + 4, :] for i in range(4)], axis=1)
        out_ref[...] = sums[:, 0:3341]

    cache_out.wait()
    rows_out.wait()
    for copy in pair + hops[0] + hops[1] + hops[2]:
        copy.wait_send()
    pltpu.make_async_copy(val.at[whole, :], val.at[whole, :], grad_send).wait()


def store_kernel(*refs):
    held, sems = refs[14:21], refs[21]
    inward = [pltpu.make_async_copy(refs[i], held[i], sems.at[0, i]) for i in range(7)]
    outward = [pltpu.make_async_copy(held[i], refs[7 + i], sems.at[1, i]) for i in range(7)]
    for copy in inward:
        copy.start()
    for i in range(7):
        inward[i].wait()
        outward[i].start()
    for copy in outward:
        copy.wait()


def store(*arrays):
    anywhere = pl.BlockSpec(memory_space=pl.ANY)
    return pl.pallas_call(
        store_kernel,
        name="store",
        out_shape=tuple(jax.ShapeDtypeStruct(a.shape, a.dtype) for a in arrays),
        in_specs=[anywhere] * 7,
        out_specs=(anywhere,) * 7,
        scratch_shapes=[pltpu.VMEM(a.shape, a.dtype) for a in arrays]
        + [pltpu.SemaphoreType.DMA((2, 7))],
        compiler_params=pltpu.CompilerParams(vmem_limit_bytes=62 * 2**20),
    )(*arrays)


def train_step(*operands):
    vmem = pl.BlockSpec(memory_space=pltpu.VMEM)
    anywhere = pl.BlockSpec(memory_space=pl.ANY)
    tail = pl.BlockSpec((128, 512), lambda i: (26, 0), memory_space=pltpu.VMEM)
    bf16, f32, i32 = jnp.bfloat16, jnp.float32, jnp.int32
    dense_out = jax.ShapeDtypeStruct((4, 3341), f32)
    dma = pltpu.SemaphoreType.DMA
    return pl.pallas_call(
        step_kernel,
        name="train_step",
        out_shape=(
            jax.ShapeDtypeStruct((4096, 128), bf16),
            jax.ShapeDtypeStruct((32, 128), f32),
            jax.ShapeDtypeStruct((32, 128), f32),
            jax.ShapeDtypeStruct((2048, 128), f32),
            dense_out,
            dense_out,
            dense_out,
        ),
        grid=(1,),
        in_specs=[vmem] * 6 + [anywhere] + [vmem] * 2 + [anywhere] * 3 + [tail] * 3 + [vmem] * 3,
        out_specs=(anywhere, vmem, vmem, anywhere, vmem, vmem, vmem),
        scratch_shapes=[
            pltpu.VMEM((4096, 128), bf16),
            pltpu.VMEM((4096, 128), bf16),
            pltpu.VMEM((2048, 128), f32),
            pltpu.VMEM((3, 14, 256, 512), bf16),
            pltpu.VMEM((1, 3584), f32),
            pltpu.VMEM((128, 1, 128), i32),
            pltpu.VMEM((128, 1, 128), i32),
            pltpu.VMEM((128, 128), i32),
            pltpu.VMEM((4096, 128), bf16),
            pltpu.VMEM((4096, 128), bf16),
            pltpu.VMEM((4096, 128), bf16),
            pltpu.VMEM((1024, 512), bf16),
            pltpu.VMEM((4096, 128), i32),
            pltpu.VMEM((16, 128), i32),
            pltpu.VMEM((2048, 128), i32),
            pltpu.VMEM((2048, 128), f32),
            pltpu.VMEM((1024, 256), bf16),
            pltpu.VMEM((28, 256, 128), f32),
            pltpu.VMEM((3, 256, 3584), bf16),
            pltpu.VMEM((3, 256, 3584), bf16),
            pltpu.VMEM((256, 512), bf16),
            pltpu.VMEM((256, 512), bf16),
            pltpu.VMEM((256, 512), bf16),
            pltpu.VMEM((6656, 256), bf16),
            pltpu.VMEM((2048, 256), bf16),
            pltpu.VMEM((4096, 256), bf16),
            pltpu.VMEM((3, 256, 256), bf16),
            pltpu.VMEM((3, 256, 256), bf16),
            pltpu.VMEM((3, 256, 256), bf16),
            pltpu.VMEM((3, 3, 7, 64, 512), bf16),
            pltpu.VMEM((3, 64, 3584), bf16),
            pltpu.VMEM((3, 3, 16, 3584), bf16),
            pltpu.VMEM((3, 4, 16, 896), bf16),
            pltpu.VMEM((3, 3, 16, 896), bf16),
            dma((3, 13)),
            dma((3,)),
            dma,
            dma,
            dma,
            dma((4,)),
            dma((3, 2)),
            dma((3, 2)),
            dma,
            dma,
            dma((3, 3, 3)),
            dma((3, 3, 3)),
        ],
        compiler_params=pltpu.CompilerParams(
            collective_id=0, has_side_effects=True, vmem_limit_bytes=62 * 2**20
        ),
    )(*operands)


def on_device(
    dense_feats,
    labels,
    slot_ids,
    needed_owner,
    needed_local,
    evicted,
    table_rows,
    table_scale,
    table_acc,
    cross_down,
    cross_up,
    cross_bias,
    hidden_weight,
    hidden_bias,
    out_weight,
):
    up_t = cross_up.T
    results = train_step(
        needed_owner.reshape(1, 2048),
        needed_local.reshape(1, 2048),
        slot_ids.T,
        dense_feats.T,
        labels.reshape(1, 256),
        evicted.reshape(16, 128),
        table_rows,
        table_scale.reshape(32, 128),
        table_acc.reshape(32, 128),
        cross_down,
        up_t,
        hidden_weight,
        cross_down,
        up_t,
        hidden_weight,
        cross_bias,
        hidden_bias.reshape(1, 512),
        out_weight,
    )
    new_rows, new_scale, new_acc, cache, grad_down, grad_hidden, grad_up = store(*results)
    return (
        new_rows,
        new_scale.reshape(4096),
        new_acc.reshape(4096),
        cache,
        grad_down,
        grad_hidden,
        grad_up,
    )


def solution(mesh):
    placed = (
        P(("hst", "chip"), None),
        P(("hst", "chip")),
        P(("hst", "chip"), None),
        P(("hst", "chip"), None),
        P(("hst", "chip")),
        P(("hst", "chip")),
        P(("hst", "chip"), None),
        P(("hst", "chip")),
        P(("hst", "chip")),
        P(),
        P(),
        P(),
        P(),
        P(),
        P(),
    )
    return jax.shard_map(
        on_device,
        mesh=mesh,
        in_specs=placed,
        out_specs=(
            P(("hst", "chip"), None),
            P(("hst", "chip")),
            P(("hst", "chip")),
            P(("hst", "chip"), None),
            P(("hst", "chip"), None),
            P(("hst", "chip"), None),
            P(("hst", "chip"), None),
        ),
        check_vma=False,
    )
```

```python
import functools

import jax
import jax.experimental.pallas as pl
import jax.experimental.pallas.tpu as pltpu
import jax.numpy as jnp
from jax import lax
from jax.sharding import PartitionSpec as P

MESH = pl.DeviceIdType.MESH
LEARN_RATE = 0.1
QUANT_TOP = 4.0


def contract_last(left, right):
    return lax.dot_general(
        left, right, (((1,), (1,)), ((), ())), preferred_element_type=jnp.float32
    )


def contract_first(left, right):
    return lax.dot_general(
        left, right, (((0,), (0,)), ((), ())), preferred_element_type=jnp.float32
    )


def coords():
    host = lax.axis_index("hst")
    chip = lax.axis_index("chip")
    return host // 4, host % 4, chip // 2, chip % 2


def hosts_from(y, z):
    return [((y + d // 4) % 4) * 4 + (z + d % 4) % 4 for d in range(16)]


def chips_from(x, core):
    return [((x + d // 2) % 4) * 2 + (core + d % 2) % 2 for d in range(8)]


def neg_host(d):
    return ((4 - d // 4) % 4) * 4 + (4 - d % 4) % 4


def neg_chip(d):
    return ((4 - d // 2) % 4) * 2 + d % 2


def greet_all(barrier):
    y, z, x, core = coords()
    chips = chips_from(x, core)

    def one(d, _):
        host = ((y + d // 4) % 4) * 4 + (z + d % 4) % 4
        for e in range(8):
            if e == 0:

                @pl.when(d > 0)
                def _():
                    pl.semaphore_signal(barrier, inc=1, device_id=(host, chips[0]), device_id_type=MESH)

            else:
                pl.semaphore_signal(barrier, inc=1, device_id=(host, chips[e]), device_id_type=MESH)
        return 0

    lax.fori_loop(0, 16, one, 0)


def hot(cond):
    return jnp.where(cond, 1.0, 0.0).astype(jnp.bfloat16)


def to_column(row):
    return jnp.broadcast_to(row, (128, 128)).T


def lane_tiles(col, count):
    lane = lax.broadcasted_iota(jnp.int32, col.shape, 1)
    return jnp.concatenate([hot(col == lane + 128 * i) for i in range(count)], axis=1)


ORDERS = (("y", "z", "x"), ("z", "x", "y"), ("x", "y", "z"))
JOBS = ((0, 0, 3, 0), (0, 3, 2, 1), (0, 5, 2, 2), (1, 0, 7, 1), (2, 0, 7, 2))
DOWN, UP, HID = 0, 1, 2


def row_order(order, me):
    row = lax.broadcasted_iota(jnp.int32, (512, 512), 0)
    at = {"core": (me["core"] + (row >> 8)) & 1}
    for stage, axis in enumerate(ORDERS[order]):
        at[axis] = (me[axis] + (row >> (6 - 2 * stage))) & 3
    source = (at["y"] * 32 + at["z"] * 8 + at["x"] * 2 + at["core"]) * 4 + (row & 3)
    return hot(source == lax.broadcasted_iota(jnp.int32, (512, 512), 1))


def shifted(me, axis, step):
    to = dict(me)
    to[axis] = (me[axis] + step) % 4
    return (to["y"] * 4 + to["z"], to["x"] * 2 + to["core"])


def step_kernel(
    owner_ref,
    local_ref,
    slots_ref,
    feats_ref,
    labels_ref,
    evict_ref,
    rows_hbm,
    scale_ref,
    acc_ref,
    down_hbm,
    up_hbm,
    hid_hbm,
    down_tail,
    up_tail,
    hid_tail,
    bias_ref,
    hid_bias_ref,
    out_w_ref,
    new_rows_hbm,
    new_scale_ref,
    new_acc_ref,
    cache_hbm,
    out_down_ref,
    out_hid_ref,
    out_up_ref,
    rows_ref,
    new_rows_ref,
    cache_ref,
    weights,
    bias,
    req,
    inc,
    asked_ref,
    val,
    ret,
    rcv,
    table2,
    qcol,
    pos,
    poscol,
    fetched,
    fetched2,
    factor,
    wides,
    rights,
    low_ref,
    grad_hid_ref,
    grad_low_ref,
    split,
    placed,
    spread,
    mine,
    theirs,
    lefts,
    first,
    second_src,
    second,
    third_src,
    third,
    load_sems,
    side_sems,
    req_send,
    req_recv,
    val_send,
    val_recv,
    pair_send,
    pair_recv,
    grad_send,
    grad_recv,
    sum_send,
    sum_recv,
):
    y, z, x, core = coords()
    me = {"y": y, "z": z, "x": x, "core": core}
    chips = chips_from(x, core)
    partner = (y * 4 + z, x * 2 + 1 - core)
    barrier = pltpu.get_barrier_semaphore()
    greet_all(barrier)
    base, crossed, mix = wides.at[0], wides.at[1], wides.at[2]

    rows_load = pltpu.make_async_copy(rows_hbm, rows_ref, side_sems.at[0])
    rows_load.start()
    loads = []
    for i, src in enumerate((down_hbm, up_hbm, hid_hbm)):
        some = []
        for j in range(13):
            copy = pltpu.make_async_copy(
                src.at[pl.ds(256 * j, 256), :], weights.at[i, j], load_sems.at[i, j]
            )
            copy.start()
            some.append(copy)
        loads.append(some)

    owner = owner_ref[...]
    far_x = ((owner >> 1) - x) & 3
    other = (owner - core) & 1
    rel = (
        (((owner >> 5) - y - far_x) & 3) * 32
        + (((owner >> 3) - z - far_x - 2 * other) & 3) * 8
        + far_x * 2
        + other
    )
    sub = lax.broadcasted_iota(jnp.int32, (128, 256), 0)
    upper = hot(
        lax.broadcasted_iota(jnp.int32, (256, 256), 0)
        < lax.broadcasted_iota(jnp.int32, (256, 256), 1)
    )
    seen = jnp.zeros((128, 1), jnp.float32)
    hi_sum = jnp.zeros((128, 32), jnp.float32)
    lo_sum = jnp.zeros((128, 32), jnp.float32)
    for i in range(8):
        part = rel[:, 256 * i : 256 * i + 256]
        hits = hot(part == sub)
        before = jnp.dot(hits, upper, preferred_element_type=jnp.float32) + seen
        wide = hits.astype(jnp.float32)
        place = jnp.sum(wide * before, axis=0, keepdims=True).astype(jnp.int32)
        seen = seen + jnp.sum(wide, axis=1, keepdims=True)
        where = part * 32 + place
        pos[2 * i : 2 * i + 1, :] = where[:, 0:128]
        pos[2 * i + 1 : 2 * i + 2, :] = where[:, 128:256]
        code = local_ref[:, 256 * i : 256 * i + 256] + 1
        here = place == lax.broadcasted_iota(jnp.int32, (32, 256), 0)
        hi = jnp.where(here, (code >> 6).astype(jnp.float32), 0.0).astype(jnp.bfloat16)
        lo = jnp.where(here, (code & 63).astype(jnp.float32), 0.0).astype(jnp.bfloat16)
        hi_sum = hi_sum + contract_last(hits, hi)
        lo_sum = lo_sum + contract_last(hits, lo)
    asked = (hi_sum * 64.0 + lo_sum).astype(jnp.int32) - 1
    asked = jnp.concatenate([asked, jnp.full((128, 96), -1, jnp.int32)], axis=1)
    for k in range(128):
        req[k] = asked[k : k + 1, :]
    inc[0] = req[0]

    pl.semaphore_wait(barrier, 127)

    def hosts_of(d):
        along_y = [((y + d // 4 + i) % 4) * 4 for i in range(4)]
        along_z = [(z + d % 4 + i) % 4 for i in range(4)]
        return [along_y[e // 2] + along_z[(e // 2 + 2 * (e % 2)) % 4] for e in range(8)]

    def ask(d, _):
        hosts = hosts_of(d)
        back = ((4 - d // 4) % 4) * 4 + (4 - d % 4) % 4
        for e in range(8):

            def go():
                pltpu.make_async_remote_copy(
                    src_ref=req.at[d * 8 + e],
                    dst_ref=inc.at[back * 8 + neg_chip(e)],
                    send_sem=req_send,
                    recv_sem=req_recv,
                    device_id=(hosts[e], chips[e]),
                    device_id_type=MESH,
                ).start()

            if e == 0:
                pl.when(d > 0)(go)
            else:
                go()
        return 0

    lax.fori_loop(0, 16, ask, 0)

    rows_load.wait()
    for i in range(32):
        rows = rows_ref[128 * i : 128 * i + 128, :].astype(jnp.float32)
        col = to_column(scale_ref[i : i + 1, :])
        table2[
            (i % 8) * 128 : (i % 8) * 128 + 128, (i // 8) * 128 : (i // 8) * 128 + 128
        ] = (rows * col).astype(jnp.bfloat16)
    for i in range(16):
        poscol[128 * i : 128 * i + 128, :] = to_column(pos[i : i + 1, :])
    ids = jnp.concatenate([slots_ref[...], jnp.zeros((102, 256), jnp.int32)], axis=0).T
    ids = ids.astype(jnp.float32)
    for t in range(26):
        factor[t] = jnp.broadcast_to(ids[:, t : t + 1], (256, 128))
    feats = jnp.concatenate(
        [feats_ref[...].astype(jnp.float32), jnp.zeros((115, 256), jnp.float32)], axis=0
    )
    base[:, 3328:3456] = feats.T.astype(jnp.bfloat16)
    base[:, 3456:3584] = jnp.zeros((256, 128), jnp.bfloat16)
    bias[...] = jnp.zeros((1, 3584), jnp.float32)
    bias[:, 0:3341] = bias_ref[...].reshape(1, 3341)
    inside = lax.broadcasted_iota(jnp.int32, (128, 512), 0) < 13
    for i, tail in enumerate((down_tail, up_tail, hid_tail)):
        weights[i, 13, 0:128, :] = jnp.where(inside, tail[...].astype(jnp.float32), 0.0).astype(
            jnp.bfloat16
        )
        weights[i, 13, 128:256, :] = jnp.zeros((128, 512), jnp.bfloat16)

    pltpu.make_async_copy(req.at[pl.ds(0, 127)], req.at[pl.ds(0, 127)], req_send).wait()
    pltpu.make_async_copy(inc.at[pl.ds(1, 127)], inc.at[pl.ds(1, 127)], req_recv).wait()
    got = inc[...].reshape(128, 128)
    asked_ref[...] = got
    got_t = got.T
    for k in range(128):
        qcol[32 * k : 32 * k + 32, :] = jnp.broadcast_to(got_t[0:32, k : k + 1], (32, 128))

    def send_blocks(d, skip_self, src, dst, send_sem, recv_sem):
        start = pl.multiple_of(d * 256, 256)
        hosts = hosts_of(d)
        back = ((4 - d // 4) % 4) * 4 + (4 - d % 4) % 4
        for e in range(8):

            def go():
                pltpu.make_async_remote_copy(
                    src_ref=src.at[pl.ds(pl.multiple_of(start + 32 * e, 32), 32), :],
                    dst_ref=dst.at[pl.ds(pl.multiple_of(back * 256 + 32 * neg_chip(e), 32), 32), :],
                    send_sem=send_sem,
                    recv_sem=recv_sem(back // 4),
                    device_id=(hosts[e], chips[e]),
                    device_id_type=MESH,
                ).start()

            if e == 0 and skip_self:
                pl.when(d > 0)(go)
            else:
                go()

    def serve(i, _):
        at = pl.multiple_of(i * 512, 512)
        query = qcol[pl.ds(at, 512), :]
        found = jnp.dot(
            lane_tiles(query & 1023, 8), table2[...], preferred_element_type=jnp.float32
        )
        quarter = query >> 10
        result = jnp.zeros((512, 128), jnp.float32)
        for q in range(4):
            result = jnp.where(quarter == q, found[:, 128 * q : 128 * q + 128], result)
        val[pl.ds(at, 512), :] = result.astype(jnp.bfloat16)
        send_blocks(2 * i, True, val, ret, val_send, lambda c: val_recv.at[c])
        send_blocks(2 * i + 1, False, val, ret, val_send, lambda c: val_recv.at[c])
        return 0

    lax.fori_loop(0, 8, serve, 0)
    ret[0:32, :] = val[0:32, :]
    for chunk in (0, 3, 2, 1):
        if chunk == 0:
            landed = ret.at[pl.ds(32, 992), :]
        else:
            landed = ret.at[pl.ds(1024 * chunk, 1024), :]
        pltpu.make_async_copy(landed, landed, val_recv.at[chunk]).wait()
        sides = jnp.concatenate(
            [
                ret[1024 * chunk : 1024 * chunk + 512, :],
                ret[1024 * chunk + 512 : 1024 * chunk + 1024, :],
            ],
            axis=1,
        )

        def pick(i, _):
            at = pl.multiple_of(i * 512, 512)
            where = poscol[pl.ds(at, 512), :]
            found = jnp.dot(lane_tiles(where & 511, 4), sides, preferred_element_type=jnp.float32)
            half = where >> 9
            if chunk == 0:
                result = jnp.zeros((512, 128), jnp.float32)
            else:
                result = fetched[pl.ds(at, 512), :]
            result = jnp.where(half == 2 * chunk, found[:, :128], result)
            fetched[pl.ds(at, 512), :] = jnp.where(half == 2 * chunk + 1, found[:, 128:], result)
            return 0

        lax.fori_loop(0, 4, pick, 0)
    fetched2[:, 0:128] = fetched[0:1024, :].astype(jnp.bfloat16)
    fetched2[:, 128:256] = fetched[1024:2048, :].astype(jnp.bfloat16)

    def fill(i, _):
        slot = factor[pl.ds(2 * i, 2)].reshape(512, 128).astype(jnp.int32)
        found = jnp.dot(
            lane_tiles(slot & 1023, 8), fetched2[...], preferred_element_type=jnp.float32
        )
        result = jnp.where(slot < 1024, found[:, :128], found[:, 128:]).astype(jnp.bfloat16)
        base[:, pl.ds(pl.multiple_of(256 * i, 128), 128)] = result[0:256]
        base[:, pl.ds(pl.multiple_of(256 * i + 128, 128), 128)] = result[256:512]
        return 0

    lax.fori_loop(0, 13, fill, 0)

    def give(slot, src, dst):
        copy = pltpu.make_async_remote_copy(
            src_ref=src,
            dst_ref=dst,
            send_sem=pair_send.at[slot],
            recv_sem=pair_recv.at[slot],
            device_id=partner,
            device_id_type=MESH,
        )
        copy.start()
        return copy

    def ordered(job, values):
        order = row_order(JOBS[job][3], me)
        mine[job] = contract_last(order[0:256], values).astype(jnp.bfloat16)
        theirs[job] = contract_last(order[256:512], values).astype(jnp.bfloat16)
        return give(3 + job, theirs.at[job], lefts.at[job])

    pair = {0: give(0, base, rights.at[0])}
    for copy in loads[DOWN]:
        copy.wait()
    low = jnp.dot(
        base[...], weights[DOWN].reshape(3584, 512), preferred_element_type=jnp.float32
    ).astype(jnp.bfloat16)
    low_ref[...] = low
    for copy in loads[UP]:
        copy.wait()

    def cross(j, _):
        cols = pl.ds(pl.multiple_of(j * 256, 256), 256)
        mixing = contract_last(low_ref[...], weights[UP, j]) + bias[:, cols]
        wide = base[:, cols].astype(jnp.float32)
        crossed[:, cols] = (wide * mixing + wide).astype(jnp.bfloat16)
        factor[2 * j] = mixing[:, 0:128] + 1.0
        factor[2 * j + 1] = mixing[:, 128:256] + 1.0
        return 0

    lax.fori_loop(0, 14, cross, 0)
    pair[1] = give(1, crossed, rights.at[1])
    pair[7] = ordered(4, low_ref[...])
    for copy in loads[HID]:
        copy.wait()
    preact = (
        jnp.dot(
            crossed[...], weights[HID].reshape(3584, 512), preferred_element_type=jnp.float32
        )
        + hid_bias_ref[...]
    )
    sig = jax.nn.sigmoid(preact)
    hidden = (preact * sig).astype(jnp.bfloat16).astype(jnp.float32)
    out_w = out_w_ref[...].astype(jnp.float32).reshape(1, 512)
    logits = jnp.sum(hidden * out_w, axis=1, keepdims=True)
    labels = labels_ref[...].astype(jnp.float32)
    labels = jnp.concatenate([to_column(labels[:, 0:128]), to_column(labels[:, 128:256])], axis=0)
    grad_logit = jax.nn.sigmoid(logits) - labels[:, 0:1]
    grad_hid_ref[...] = (grad_logit * out_w * (sig * (1.0 + preact * (1.0 - sig)))).astype(
        jnp.bfloat16
    )
    pair[6] = ordered(3, grad_hid_ref[...])

    def back(j, _):
        cols = pl.ds(pl.multiple_of(j * 256, 256), 256)
        grad_cross = contract_last(grad_hid_ref[...], weights[HID, j])
        mix[:, cols] = (grad_cross * base[:, cols].astype(jnp.float32)).astype(jnp.bfloat16)
        factor[2 * j] = grad_cross[:, 0:128] * factor[2 * j]
        factor[2 * j + 1] = grad_cross[:, 128:256] * factor[2 * j + 1]
        return 0

    lax.fori_loop(0, 14, back, 0)
    pair[2] = give(2, mix, rights.at[2])
    grad_low_ref[...] = jnp.dot(
        mix[...], weights[UP].reshape(3584, 512), preferred_element_type=jnp.float32
    ).astype(jnp.bfloat16)
    for job in range(3):
        pair[3 + job] = ordered(job, grad_low_ref[...])

    room = ((UP, 0), (HID, 0), (HID, 7))

    def hop(job, axis, step, sem, src, dst):
        copy = pltpu.make_async_remote_copy(
            src_ref=src,
            dst_ref=dst,
            send_sem=sum_send.at[job, sem],
            recv_sem=sum_recv.at[job, sem],
            device_id=shifted(me, axis, step),
            device_id_type=MESH,
        )
        copy.start()
        return copy

    hops = [[] for _ in JOBS]

    def multiply(job):
        a, start, count, order = JOBS[job]
        axis = ORDERS[order][0]
        place, at = room[a]
        if start == 0:
            pair[a].wait_recv()
        pair[3 + job].wait_recv()

        def product(j, _):
            cols = pl.ds(pl.multiple_of(j * 512, 512), 512)
            both = jnp.concatenate([mine[job], lefts[job]], axis=1)
            wide = jnp.concatenate([wides[a, :, cols], rights[a, :, cols]], axis=0)
            weights[place, at + j] = jnp.dot(both, wide, preferred_element_type=jnp.float32).astype(
                jnp.bfloat16
            )
            return 0

        lax.fori_loop(start, start + count, product, 0)
        blocks = pl.ds(at + start, count)
        to = pl.ds(start, count)

        def rows(first_row):
            return weights.at[place, blocks, pl.ds(first_row, 32), :]

        upper, lower = pl.ds(0, 32), pl.ds(32, 32)
        hops[job] = [
            hop(job, axis, 1, 0, rows(128), first.at[a, 2, to, upper, :]),
            hop(job, axis, 3, 1, rows(160), first.at[a, 2, to, lower, :]),
            hop(job, axis, 1, 2, rows(96), first.at[a, 0, to, lower, :]),
            hop(job, axis, 3, 3, rows(192), first.at[a, 1, to, upper, :]),
        ]

    def relay(job):
        a, start, count, order = JOBS[job]
        axis = ORDERS[order][0]
        place, at = room[a]
        blocks = pl.ds(at + start, count)
        to = pl.ds(start, count)
        for step, sem, row, part in ((1, 0, 64, 0), (3, 1, 224, 1)):
            hops[job][sem].wait_recv()
            side = pl.ds(32 * part, 32)

            def add(j, _):
                own = weights[place, at + j, row : row + 32, :].astype(jnp.float32)
                came = first[a, 2, j, 32 * part : 32 * part + 32, :].astype(jnp.float32)
                weights[place, at + j, row : row + 32, :] = (own + came).astype(jnp.bfloat16)
                return 0

            lax.fori_loop(start, start + count, add, 0)
            hops[job].append(
                hop(
                    job,
                    axis,
                    step,
                    4 + part,
                    weights.at[place, blocks, pl.ds(row, 32), :],
                    first.at[a, part, to, side, :],
                )
            )

    multiply(3)
    multiply(4)

    def last(j, _):
        grad = contract_last(grad_low_ref[...], weights[DOWN, j])
        for side in range(2):
            t = 2 * j + side
            wide = grad[:, 128 * side : 128 * side + 128] + factor[t]
            here = pl.ds(pl.multiple_of(t * 256, 256), 256)
            split[here, :] = jnp.concatenate([wide, wide], axis=1).astype(jnp.bfloat16)
        return 0

    lax.fori_loop(0, 13, last, 0)
    relay(3)
    for job in range(3):
        multiply(job)
    relay(4)
    ids = jnp.concatenate([slots_ref[...], jnp.zeros((102, 256), jnp.int32)], axis=0).T
    for t in range(26):
        half = jnp.broadcast_to(ids[:, t : t + 1] >> 10, (256, 128))
        low_side = split[256 * t : 256 * t + 256, 0:128].astype(jnp.float32)
        split[256 * t : 256 * t + 256, 0:128] = jnp.where(half == 0, low_side, 0.0).astype(
            jnp.bfloat16
        )
        split[256 * t : 256 * t + 256, 128:256] = jnp.where(half == 1, low_side, 0.0).astype(
            jnp.bfloat16
        )

    def slots(m, _):
        at = pl.multiple_of(m * 256, 256)
        slot = lax.broadcasted_iota(jnp.int32, (256, 256), 0) + at
        picks = jnp.concatenate(
            [hot(slot == (slots_ref[t : t + 1, :] & 1023)) for t in range(26)], axis=1
        )
        sums = jnp.dot(picks, split[...], preferred_element_type=jnp.float32)
        for side in range(2):
            for block in range(2):
                i = side * 8 + m * 2 + block
                here = pl.ds(pl.multiple_of(i * 128, 128), 128)
                total = sums[128 * block : 128 * block + 128, 128 * side : 128 * side + 128]
                gone = to_column(evict_ref[pl.ds(i, 1), :].astype(jnp.float32))
                cache_ref[here, :] = total * (1.0 - gone)
                sent = total * gone
                upper = poscol[here, :] >> 11
                placed[here, 0:128] = jnp.where(upper == 0, sent, 0.0).astype(jnp.bfloat16)
                placed[here, 128:256] = jnp.where(upper == 1, sent, 0.0).astype(jnp.bfloat16)
        return 0

    lax.fori_loop(0, 4, slots, 0)
    for job in range(3):
        relay(job)
    cache_out = pltpu.make_async_copy(cache_ref, cache_hbm, side_sems.at[1])
    cache_out.start()
    whole = pl.ds(32, 4064)
    pltpu.make_async_copy(val.at[whole, :], val.at[whole, :], val_send).wait()

    def send(j, _):
        at = pl.multiple_of(j * 512, 512)
        place = lax.broadcasted_iota(jnp.int32, (512, 128), 0) + at
        picks = jnp.concatenate(
            [hot(place == (pos[i : i + 1, :] & 2047)) for i in range(16)], axis=1
        )
        sums = jnp.dot(picks, placed[...], preferred_element_type=jnp.float32)
        for side in range(2):
            val[pl.ds(pl.multiple_of(at + 2048 * side, 512), 512), :] = sums[
                :, 128 * side : 128 * side + 128
            ].astype(jnp.bfloat16)
            for more in range(2):
                send_blocks(
                    2 * j + more + 8 * side,
                    side == 0 and more == 0,
                    val,
                    rcv,
                    grad_send,
                    lambda c: grad_recv,
                )
        return 0

    lax.fori_loop(0, 4, send, 0)
    rcv[0:32, :] = val[0:32, :]

    for job in (3, 4, 0, 1, 2):
        a, start, count, order = JOBS[job]
        place, at = room[a]
        for copy in hops[job][2:6]:
            copy.wait_recv()

        def gather(j, _):
            sums = weights[place, at + j, 0:64, :].astype(jnp.float32)
            for side in range(2):
                sums = sums + first[a, side, j].astype(jnp.float32)
            second_src[a, :, pl.ds(pl.multiple_of(j * 512, 512), 512)] = sums.astype(jnp.bfloat16)
            return 0

        lax.fori_loop(start, start + count, gather, 0)
        cols = pl.ds(start * 512, count * 512)
        for step in (2, 1, 3):
            src = second_src.at[a, pl.ds(16 * step, 16), cols]
            dst = second.at[a, step - 1, :, cols]
            hops[job].append(hop(job, ORDERS[order][1], step, 5 + step, src, dst))

    pltpu.make_async_copy(rcv.at[whole, :], rcv.at[whole, :], grad_recv).wait()
    for k in range(128):
        g, c = k % 32, k // 32
        half = qcol[32 * k : 32 * k + 32, :] >> 11
        grad = rcv[32 * k : 32 * k + 32, :].astype(jnp.float32)
        at = (g * 4 + c) * 32
        spread[at : at + 32, 0:128] = jnp.where(half == 0, grad, 0.0).astype(jnp.bfloat16)
        spread[at : at + 32, 128:256] = jnp.where(half == 1, grad, 0.0).astype(jnp.bfloat16)
    asked = asked_ref[...]
    asked = jnp.concatenate([asked[32 * c : 32 * c + 32, 0:32] for c in range(4)], axis=1) & 2047

    def update(m, _):
        at = pl.multiple_of(m * 256, 256)
        row = lax.broadcasted_iota(jnp.int32, (256, 128), 0) + at
        picks = jnp.concatenate([hot(row == asked[g : g + 1, :]) for g in range(32)], axis=1)
        sums = jnp.dot(picks, spread[...], preferred_element_type=jnp.float32)
        for side in range(2):
            for block in range(2):
                i = side * 16 + m * 2 + block
                here = pl.ds(pl.multiple_of(i * 128, 128), 128)
                row_grad = sums[128 * block : 128 * block + 128, 128 * side : 128 * side + 128]
                acc = to_column(acc_ref[pl.ds(i, 1), :])
                acc = acc + jnp.sum(row_grad * row_grad, axis=1, keepdims=True) * (1.0 / 128.0)
                new_acc_ref[pl.ds(i, 1), :] = acc.T[0:1, :]
                values = rows_ref[here, :].astype(jnp.float32) * to_column(scale_ref[pl.ds(i, 1), :])
                values = values - LEARN_RATE * row_grad / jnp.sqrt(acc)
                top = jnp.max(jnp.abs(values), axis=1, keepdims=True)
                scale = (jnp.broadcast_to(top, (128, 128)) + 1e-06) / QUANT_TOP
                new_scale_ref[pl.ds(i, 1), :] = scale.T[0:1, :]
                new_rows_ref[here, :] = (values / scale).astype(jnp.bfloat16)
        return 0

    lax.fori_loop(0, 4, update, 0)

    for job in (3, 4, 0, 1, 2):
        a, start, count, order = JOBS[job]
        cols = slice(start * 512, (start + count) * 512)
        wide = count * 128
        for copy in hops[job][6:]:
            copy.wait_recv()
        sums = second_src[a, 0:16, cols].astype(jnp.float32)
        for step in range(3):
            sums = sums + second[a, step, :, cols].astype(jnp.float32)
        for step in range(4):
            piece = sums[4 * step : 4 * step + 4, :]
            third_src[a, step, :, start * 128 : start * 128 + wide] = jnp.concatenate(
                [piece[:, wide * i : wide * i + wide] for i in range(4)], axis=0
            ).astype(jnp.bfloat16)
        narrow = pl.ds(start * 128, wide)
        for step in (2, 1, 3):
            src = third_src.at[a, step, :, narrow]
            dst = third.at[a, step - 1, :, narrow]
            hops[job].append(hop(job, ORDERS[order][2], step, 8 + step, src, dst))

    lax.fori_loop(4, 8, update, 0)
    rows_out = pltpu.make_async_copy(new_rows_ref, new_rows_hbm, side_sems.at[2])
    rows_out.start()

    out_refs = (out_down_ref, out_hid_ref, out_up_ref)
    for job in (3, 4, 0, 1, 2):
        a, start, count, order = JOBS[job]
        for copy in hops[job][9:]:
            copy.wait_recv()
        cols = slice(start * 128, (start + count) * 128)
        sums = third_src[a, 0, :, cols].astype(jnp.float32)
        for step in range(3):
            sums = sums + third[a, step, :, cols].astype(jnp.float32)
        sums = sums * (1.0 / 128.0)
        sums = jnp.concatenate([sums[4 * i : 4 * i + 4, :] for i in range(4)], axis=1)
        end = min(3341, (start + count) * 512)
        out_refs[a][:, start * 512 : end] = sums[:, 0 : end - start * 512]

    cache_out.wait()
    rows_out.wait()
    for copy in list(pair.values()) + [copy for some in hops for copy in some]:
        copy.wait_send()
    pltpu.make_async_copy(val.at[whole, :], val.at[whole, :], grad_send).wait()


def store_kernel(*refs):
    held, sems = refs[14:21], refs[21]
    inward = [pltpu.make_async_copy(refs[i], held[i], sems.at[0, i]) for i in range(7)]
    outward = [pltpu.make_async_copy(held[i], refs[7 + i], sems.at[1, i]) for i in range(7)]
    for copy in inward:
        copy.start()
    for i in range(7):
        inward[i].wait()
        outward[i].start()
    for copy in outward:
        copy.wait()


def store(*arrays):
    anywhere = pl.BlockSpec(memory_space=pl.ANY)
    return pl.pallas_call(
        store_kernel,
        name="store",
        out_shape=tuple(jax.ShapeDtypeStruct(a.shape, a.dtype) for a in arrays),
        in_specs=[anywhere] * 7,
        out_specs=(anywhere,) * 7,
        scratch_shapes=[pltpu.VMEM(a.shape, a.dtype) for a in arrays]
        + [pltpu.SemaphoreType.DMA((2, 7))],
        compiler_params=pltpu.CompilerParams(vmem_limit_bytes=62 * 2**20),
    )(*arrays)


def train_step(*operands):
    vmem = pl.BlockSpec(memory_space=pltpu.VMEM)
    anywhere = pl.BlockSpec(memory_space=pl.ANY)
    tail = pl.BlockSpec((128, 512), lambda i: (26, 0), memory_space=pltpu.VMEM)
    bf16, f32, i32 = jnp.bfloat16, jnp.float32, jnp.int32
    dense_out = jax.ShapeDtypeStruct((4, 3341), f32)
    dma = pltpu.SemaphoreType.DMA
    return pl.pallas_call(
        step_kernel,
        name="train_step",
        out_shape=(
            jax.ShapeDtypeStruct((4096, 128), bf16),
            jax.ShapeDtypeStruct((32, 128), f32),
            jax.ShapeDtypeStruct((32, 128), f32),
            jax.ShapeDtypeStruct((2048, 128), f32),
            dense_out,
            dense_out,
            dense_out,
        ),
        grid=(1,),
        in_specs=[vmem] * 6 + [anywhere] + [vmem] * 2 + [anywhere] * 3 + [tail] * 3 + [vmem] * 3,
        out_specs=(anywhere, vmem, vmem, anywhere, vmem, vmem, vmem),
        scratch_shapes=[
            pltpu.VMEM((4096, 128), bf16),
            pltpu.VMEM((4096, 128), bf16),
            pltpu.VMEM((2048, 128), f32),
            pltpu.VMEM((3, 14, 256, 512), bf16),
            pltpu.VMEM((1, 3584), f32),
            pltpu.VMEM((128, 1, 128), i32),
            pltpu.VMEM((128, 1, 128), i32),
            pltpu.VMEM((128, 128), i32),
            pltpu.VMEM((4096, 128), bf16),
            pltpu.VMEM((4096, 128), bf16),
            pltpu.VMEM((4096, 128), bf16),
            pltpu.VMEM((1024, 512), bf16),
            pltpu.VMEM((4096, 128), i32),
            pltpu.VMEM((16, 128), i32),
            pltpu.VMEM((2048, 128), i32),
            pltpu.VMEM((2048, 128), f32),
            pltpu.VMEM((1024, 256), bf16),
            pltpu.VMEM((28, 256, 128), f32),
            pltpu.VMEM((3, 256, 3584), bf16),
            pltpu.VMEM((3, 256, 3584), bf16),
            pltpu.VMEM((256, 512), bf16),
            pltpu.VMEM((256, 512), bf16),
            pltpu.VMEM((256, 512), bf16),
            pltpu.VMEM((6656, 256), bf16),
            pltpu.VMEM((2048, 256), bf16),
            pltpu.VMEM((4096, 256), bf16),
            pltpu.VMEM((5, 256, 256), bf16),
            pltpu.VMEM((5, 256, 256), bf16),
            pltpu.VMEM((5, 256, 256), bf16),
            pltpu.VMEM((3, 3, 7, 64, 512), bf16),
            pltpu.VMEM((3, 64, 3584), bf16),
            pltpu.VMEM((3, 3, 16, 3584), bf16),
            pltpu.VMEM((3, 4, 16, 896), bf16),
            pltpu.VMEM((3, 3, 16, 896), bf16),
            dma((3, 13)),
            dma((3,)),
            dma,
            dma,
            dma,
            dma((4,)),
            dma((8,)),
            dma((8,)),
            dma,
            dma,
            dma((5, 12)),
            dma((5, 12)),
        ],
        compiler_params=pltpu.CompilerParams(
            collective_id=0, has_side_effects=True, vmem_limit_bytes=62 * 2**20
        ),
    )(*operands)


def on_device(
    dense_feats,
    labels,
    slot_ids,
    needed_owner,
    needed_local,
    evicted,
    table_rows,
    table_scale,
    table_acc,
    cross_down,
    cross_up,
    cross_bias,
    hidden_weight,
    hidden_bias,
    out_weight,
):
    up_t = cross_up.T
    results = train_step(
        needed_owner.reshape(1, 2048),
        needed_local.reshape(1, 2048),
        slot_ids.T,
        dense_feats.T,
        labels.reshape(1, 256),
        evicted.reshape(16, 128),
        table_rows,
        table_scale.reshape(32, 128),
        table_acc.reshape(32, 128),
        cross_down,
        up_t,
        hidden_weight,
        cross_down,
        up_t,
        hidden_weight,
        cross_bias,
        hidden_bias.reshape(1, 512),
        out_weight,
    )
    new_rows, new_scale, new_acc, cache, grad_down, grad_hidden, grad_up = store(*results)
    return (
        new_rows,
        new_scale.reshape(4096),
        new_acc.reshape(4096),
        cache,
        grad_down,
        grad_hidden,
        grad_up,
    )


def solution(mesh):
    placed = (
        P(("hst", "chip"), None),
        P(("hst", "chip")),
        P(("hst", "chip"), None),
        P(("hst", "chip"), None),
        P(("hst", "chip")),
        P(("hst", "chip")),
        P(("hst", "chip"), None),
        P(("hst", "chip")),
        P(("hst", "chip")),
        P(),
        P(),
        P(),
        P(),
        P(),
        P(),
    )
    return jax.shard_map(
        on_device,
        mesh=mesh,
        in_specs=placed,
        out_specs=(
            P(("hst", "chip"), None),
            P(("hst", "chip")),
            P(("hst", "chip")),
            P(("hst", "chip"), None),
            P(("hst", "chip"), None),
            P(("hst", "chip"), None),
            P(("hst", "chip"), None),
        ),
        check_vma=False,
    )
```

```python
import functools

import jax
import jax.experimental.pallas as pl
import jax.experimental.pallas.tpu as pltpu
import jax.numpy as jnp
from jax import lax
from jax.sharding import PartitionSpec as P

MESH = pl.DeviceIdType.MESH
LEARN_RATE = 0.1
QUANT_TOP = 4.0


def contract_last(left, right):
    return lax.dot_general(
        left, right, (((1,), (1,)), ((), ())), preferred_element_type=jnp.float32
    )


def contract_first(left, right):
    return lax.dot_general(
        left, right, (((0,), (0,)), ((), ())), preferred_element_type=jnp.float32
    )


def coords():
    host = lax.axis_index("hst")
    chip = lax.axis_index("chip")
    return host // 4, host % 4, chip // 2, chip % 2


def hosts_from(y, z):
    return [((y + d // 4) % 4) * 4 + (z + d % 4) % 4 for d in range(16)]


def chips_from(x, core):
    return [((x + d // 2) % 4) * 2 + (core + d % 2) % 2 for d in range(8)]


def neg_host(d):
    return ((4 - d // 4) % 4) * 4 + (4 - d % 4) % 4


def neg_chip(d):
    return ((4 - d // 2) % 4) * 2 + d % 2


def greet_all(barrier):
    y, z, x, core = coords()
    chips = chips_from(x, core)

    def one(d, _):
        host = ((y + d // 4) % 4) * 4 + (z + d % 4) % 4
        for e in range(8):
            if e == 0:

                @pl.when(d > 0)
                def _():
                    pl.semaphore_signal(barrier, inc=1, device_id=(host, chips[0]), device_id_type=MESH)

            else:
                pl.semaphore_signal(barrier, inc=1, device_id=(host, chips[e]), device_id_type=MESH)
        return 0

    lax.fori_loop(0, 16, one, 0)


def hot(cond):
    return jnp.where(cond, 1.0, 0.0).astype(jnp.bfloat16)


def to_column(row):
    return jnp.broadcast_to(row, (128, 128)).T


def lane_tiles(col, count):
    lane = lax.broadcasted_iota(jnp.int32, col.shape, 1)
    return jnp.concatenate([hot(col == lane + 128 * i) for i in range(count)], axis=1)


ORDERS = (("y", "z", "x"), ("z", "x", "y"), ("x", "y", "z"))
JOBS = ((0, 0, 3, 0), (0, 3, 2, 1), (0, 5, 2, 2), (1, 0, 7, 1), (2, 0, 7, 2))
DOWN, UP, HID = 0, 1, 2


def row_order(order, me):
    row = lax.broadcasted_iota(jnp.int32, (512, 512), 0)
    at = {"core": (me["core"] + (row >> 8)) & 1}
    for stage, axis in enumerate(ORDERS[order]):
        at[axis] = (me[axis] + (row >> (6 - 2 * stage))) & 3
    source = (at["y"] * 32 + at["z"] * 8 + at["x"] * 2 + at["core"]) * 4 + (row & 3)
    return hot(source == lax.broadcasted_iota(jnp.int32, (512, 512), 1))


def shifted(me, axis, step):
    to = dict(me)
    to[axis] = (me[axis] + step) % 4
    return (to["y"] * 4 + to["z"], to["x"] * 2 + to["core"])


def step_kernel(
    owner_ref,
    local_ref,
    slots_ref,
    feats_ref,
    labels_ref,
    evict_ref,
    rows_hbm,
    scale_ref,
    acc_ref,
    down_hbm,
    up_hbm,
    hid_hbm,
    down_tail,
    up_tail,
    hid_tail,
    bias_ref,
    hid_bias_ref,
    out_w_ref,
    new_rows_hbm,
    new_scale_ref,
    new_acc_ref,
    cache_hbm,
    out_down_ref,
    out_hid_ref,
    out_up_ref,
    rows_ref,
    new_rows_ref,
    cache_ref,
    weights,
    bias,
    req,
    inc,
    asked_ref,
    val,
    ret,
    rcv,
    table2,
    qcol,
    pos,
    poscol,
    fetched,
    fetched2,
    factor,
    wides,
    rights,
    low_ref,
    grad_hid_ref,
    grad_low_ref,
    split,
    placed,
    spread,
    mine,
    theirs,
    lefts,
    first,
    second_src,
    second,
    third_src,
    third,
    load_sems,
    side_sems,
    req_send,
    req_recv,
    val_send,
    val_recv,
    pair_send,
    pair_recv,
    grad_send,
    grad_recv,
    sum_send,
    sum_recv,
):
    y, z, x, core = coords()
    me = {"y": y, "z": z, "x": x, "core": core}
    chips = chips_from(x, core)
    partner = (y * 4 + z, x * 2 + 1 - core)
    barrier = pltpu.get_barrier_semaphore()
    greet_all(barrier)
    base, crossed, mix = wides.at[0], wides.at[1], wides.at[2]

    rows_load = pltpu.make_async_copy(rows_hbm, rows_ref, side_sems.at[0])
    rows_load.start()
    loads = []
    for i, src in enumerate((down_hbm, up_hbm, hid_hbm)):
        some = []
        for j in range(13):
            copy = pltpu.make_async_copy(
                src.at[pl.ds(256 * j, 256), :], weights.at[i, j], load_sems.at[i, j]
            )
            copy.start()
            some.append(copy)
        loads.append(some)

    owner = owner_ref[...]
    far_x = ((owner >> 1) - x) & 3
    other = (owner - core) & 1
    rel = (
        (((owner >> 5) - y - far_x) & 3) * 32
        + (((owner >> 3) - z - far_x - 2 * other) & 3) * 8
        + far_x * 2
        + other
    )
    sub = lax.broadcasted_iota(jnp.int32, (128, 256), 0)
    upper = hot(
        lax.broadcasted_iota(jnp.int32, (256, 256), 0)
        < lax.broadcasted_iota(jnp.int32, (256, 256), 1)
    )
    seen = jnp.zeros((128, 1), jnp.float32)
    hi_sum = jnp.zeros((128, 32), jnp.float32)
    lo_sum = jnp.zeros((128, 32), jnp.float32)
    for i in range(8):
        part = rel[:, 256 * i : 256 * i + 256]
        hits = hot(part == sub)
        before = jnp.dot(hits, upper, preferred_element_type=jnp.float32) + seen
        wide = hits.astype(jnp.float32)
        place = jnp.sum(wide * before, axis=0, keepdims=True).astype(jnp.int32)
        seen = seen + jnp.sum(wide, axis=1, keepdims=True)
        where = part * 32 + place
        pos[2 * i : 2 * i + 1, :] = where[:, 0:128]
        pos[2 * i + 1 : 2 * i + 2, :] = where[:, 128:256]
        code = local_ref[:, 256 * i : 256 * i + 256] + 1
        here = place == lax.broadcasted_iota(jnp.int32, (32, 256), 0)
        hi = jnp.where(here, (code >> 6).astype(jnp.float32), 0.0).astype(jnp.bfloat16)
        lo = jnp.where(here, (code & 63).astype(jnp.float32), 0.0).astype(jnp.bfloat16)
        hi_sum = hi_sum + contract_last(hits, hi)
        lo_sum = lo_sum + contract_last(hits, lo)
    asked = (hi_sum * 64.0 + lo_sum).astype(jnp.int32) - 1
    asked = jnp.concatenate([asked, jnp.full((128, 96), -1, jnp.int32)], axis=1)
    for k in range(128):
        req[k] = asked[k : k + 1, :]
    inc[0] = req[0]

    pl.semaphore_wait(barrier, 127)

    def hosts_of(d):
        along_y = [((y + d // 4 + i) % 4) * 4 for i in range(4)]
        along_z = [(z + d % 4 + i) % 4 for i in range(4)]
        return [along_y[e // 2] + along_z[(e // 2 + 2 * (e % 2)) % 4] for e in range(8)]

    def ask(d, _):
        hosts = hosts_of(d)
        back = ((4 - d // 4) % 4) * 4 + (4 - d % 4) % 4
        for e in range(8):

            def go():
                pltpu.make_async_remote_copy(
                    src_ref=req.at[d * 8 + e],
                    dst_ref=inc.at[back * 8 + neg_chip(e)],
                    send_sem=req_send,
                    recv_sem=req_recv,
                    device_id=(hosts[e], chips[e]),
                    device_id_type=MESH,
                ).start()

            if e == 0:
                pl.when(d > 0)(go)
            else:
                go()
        return 0

    lax.fori_loop(0, 16, ask, 0)

    rows_load.wait()
    for i in range(32):
        rows = rows_ref[128 * i : 128 * i + 128, :].astype(jnp.float32)
        col = to_column(scale_ref[i : i + 1, :])
        table2[
            (i % 8) * 128 : (i % 8) * 128 + 128, (i // 8) * 128 : (i // 8) * 128 + 128
        ] = (rows * col).astype(jnp.bfloat16)
    for i in range(16):
        poscol[128 * i : 128 * i + 128, :] = to_column(pos[i : i + 1, :])
    ids = jnp.concatenate([slots_ref[...], jnp.zeros((102, 256), jnp.int32)], axis=0).T
    ids = ids.astype(jnp.float32)
    for t in range(26):
        factor[t] = jnp.broadcast_to(ids[:, t : t + 1], (256, 128))
    feats = jnp.concatenate(
        [feats_ref[...].astype(jnp.float32), jnp.zeros((115, 256), jnp.float32)], axis=0
    )
    base[:, 3328:3456] = feats.T.astype(jnp.bfloat16)
    base[:, 3456:3584] = jnp.zeros((256, 128), jnp.bfloat16)
    bias[...] = jnp.zeros((1, 3584), jnp.float32)
    bias[:, 0:3341] = bias_ref[...].reshape(1, 3341)
    inside = lax.broadcasted_iota(jnp.int32, (128, 512), 0) < 13
    for i, tail in enumerate((down_tail, up_tail, hid_tail)):
        weights[i, 13, 0:128, :] = jnp.where(inside, tail[...].astype(jnp.float32), 0.0).astype(
            jnp.bfloat16
        )
        weights[i, 13, 128:256, :] = jnp.zeros((128, 512), jnp.bfloat16)

    pltpu.make_async_copy(req.at[pl.ds(0, 127)], req.at[pl.ds(0, 127)], req_send).wait()
    pltpu.make_async_copy(inc.at[pl.ds(1, 127)], inc.at[pl.ds(1, 127)], req_recv).wait()
    got = inc[...].reshape(128, 128)
    asked_ref[...] = got
    got_t = got.T
    for k in range(128):
        qcol[32 * k : 32 * k + 32, :] = jnp.broadcast_to(got_t[0:32, k : k + 1], (32, 128))

    def send_blocks(d, skip_self, src, dst, send_sem, recv_sem):
        start = pl.multiple_of(d * 256, 256)
        hosts = hosts_of(d)
        back = ((4 - d // 4) % 4) * 4 + (4 - d % 4) % 4
        for e in range(8):

            def go():
                pltpu.make_async_remote_copy(
                    src_ref=src.at[pl.ds(pl.multiple_of(start + 32 * e, 32), 32), :],
                    dst_ref=dst.at[pl.ds(pl.multiple_of(back * 256 + 32 * neg_chip(e), 32), 32), :],
                    send_sem=send_sem,
                    recv_sem=recv_sem(back // 4),
                    device_id=(hosts[e], chips[e]),
                    device_id_type=MESH,
                ).start()

            if e == 0 and skip_self:
                pl.when(d > 0)(go)
            else:
                go()

    def serve(i, _):
        at = pl.multiple_of(i * 512, 512)
        query = qcol[pl.ds(at, 512), :]
        found = jnp.dot(
            lane_tiles(query & 1023, 8), table2[...], preferred_element_type=jnp.float32
        )
        quarter = query >> 10
        result = jnp.zeros((512, 128), jnp.float32)
        for q in range(4):
            result = jnp.where(quarter == q, found[:, 128 * q : 128 * q + 128], result)
        val[pl.ds(at, 512), :] = result.astype(jnp.bfloat16)
        send_blocks(2 * i, True, val, ret, val_send, lambda c: val_recv.at[c])
        send_blocks(2 * i + 1, False, val, ret, val_send, lambda c: val_recv.at[c])
        return 0

    lax.fori_loop(0, 8, serve, 0)
    ret[0:32, :] = val[0:32, :]
    for chunk in (0, 3, 2, 1):
        if chunk == 0:
            landed = ret.at[pl.ds(32, 992), :]
        else:
            landed = ret.at[pl.ds(1024 * chunk, 1024), :]
        pltpu.make_async_copy(landed, landed, val_recv.at[chunk]).wait()
        sides = jnp.concatenate(
            [
                ret[1024 * chunk : 1024 * chunk + 512, :],
                ret[1024 * chunk + 512 : 1024 * chunk + 1024, :],
            ],
            axis=1,
        )

        def pick(i, _):
            at = pl.multiple_of(i * 512, 512)
            where = poscol[pl.ds(at, 512), :]
            found = jnp.dot(lane_tiles(where & 511, 4), sides, preferred_element_type=jnp.float32)
            half = where >> 9
            if chunk == 0:
                result = jnp.zeros((512, 128), jnp.float32)
            else:
                result = fetched[pl.ds(at, 512), :]
            result = jnp.where(half == 2 * chunk, found[:, :128], result)
            fetched[pl.ds(at, 512), :] = jnp.where(half == 2 * chunk + 1, found[:, 128:], result)
            return 0

        lax.fori_loop(0, 4, pick, 0)
    fetched2[:, 0:128] = fetched[0:1024, :].astype(jnp.bfloat16)
    fetched2[:, 128:256] = fetched[1024:2048, :].astype(jnp.bfloat16)

    def fill(i, _):
        slot = factor[pl.ds(2 * i, 2)].reshape(512, 128).astype(jnp.int32)
        found = jnp.dot(
            lane_tiles(slot & 1023, 8), fetched2[...], preferred_element_type=jnp.float32
        )
        result = jnp.where(slot < 1024, found[:, :128], found[:, 128:]).astype(jnp.bfloat16)
        base[:, pl.ds(pl.multiple_of(256 * i, 128), 128)] = result[0:256]
        base[:, pl.ds(pl.multiple_of(256 * i + 128, 128), 128)] = result[256:512]
        return 0

    lax.fori_loop(0, 13, fill, 0)

    def give(slot, src, dst):
        copy = pltpu.make_async_remote_copy(
            src_ref=src,
            dst_ref=dst,
            send_sem=pair_send.at[slot],
            recv_sem=pair_recv.at[slot],
            device_id=partner,
            device_id_type=MESH,
        )
        copy.start()
        return copy

    def ordered(job, values):
        order = row_order(JOBS[job][3], me)
        mine[job] = contract_last(order[0:256], values).astype(jnp.bfloat16)
        theirs[job] = contract_last(order[256:512], values).astype(jnp.bfloat16)
        return give(3 + job, theirs.at[job], lefts.at[job])

    pair = {0: give(0, base, rights.at[0])}
    for copy in loads[DOWN]:
        copy.wait()
    low = jnp.dot(
        base[...], weights[DOWN].reshape(3584, 512), preferred_element_type=jnp.float32
    ).astype(jnp.bfloat16)
    low_ref[...] = low
    for copy in loads[UP]:
        copy.wait()

    def cross(j, _):
        cols = pl.ds(pl.multiple_of(j * 256, 256), 256)
        mixing = contract_last(low_ref[...], weights[UP, j]) + bias[:, cols]
        wide = base[:, cols].astype(jnp.float32)
        crossed[:, cols] = (wide * mixing + wide).astype(jnp.bfloat16)
        factor[2 * j] = mixing[:, 0:128] + 1.0
        factor[2 * j + 1] = mixing[:, 128:256] + 1.0
        return 0

    lax.fori_loop(0, 14, cross, 0)
    pair[1] = give(1, crossed, rights.at[1])
    pair[7] = ordered(4, low_ref[...])
    for copy in loads[HID]:
        copy.wait()
    preact = (
        jnp.dot(
            crossed[...], weights[HID].reshape(3584, 512), preferred_element_type=jnp.float32
        )
        + hid_bias_ref[...]
    )
    sig = jax.nn.sigmoid(preact)
    hidden = (preact * sig).astype(jnp.bfloat16).astype(jnp.float32)
    out_w = out_w_ref[...].astype(jnp.float32).reshape(1, 512)
    logits = jnp.sum(hidden * out_w, axis=1, keepdims=True)
    labels = labels_ref[...].astype(jnp.float32)
    labels = jnp.concatenate([to_column(labels[:, 0:128]), to_column(labels[:, 128:256])], axis=0)
    grad_logit = jax.nn.sigmoid(logits) - labels[:, 0:1]
    grad_hid_ref[...] = (grad_logit * out_w * (sig * (1.0 + preact * (1.0 - sig)))).astype(
        jnp.bfloat16
    )
    pair[6] = ordered(3, grad_hid_ref[...])

    def back(j, _):
        cols = pl.ds(pl.multiple_of(j * 256, 256), 256)
        grad_cross = contract_last(grad_hid_ref[...], weights[HID, j])
        mix[:, cols] = (grad_cross * base[:, cols].astype(jnp.float32)).astype(jnp.bfloat16)
        factor[2 * j] = grad_cross[:, 0:128] * factor[2 * j]
        factor[2 * j + 1] = grad_cross[:, 128:256] * factor[2 * j + 1]
        return 0

    lax.fori_loop(0, 14, back, 0)
    pair[2] = give(2, mix, rights.at[2])
    grad_low_ref[...] = jnp.dot(
        mix[...], weights[UP].reshape(3584, 512), preferred_element_type=jnp.float32
    ).astype(jnp.bfloat16)
    for job in range(3):
        pair[3 + job] = ordered(job, grad_low_ref[...])

    room = ((UP, 0), (HID, 0), (HID, 7))

    def hop(job, axis, step, sem, src, dst):
        copy = pltpu.make_async_remote_copy(
            src_ref=src,
            dst_ref=dst,
            send_sem=sum_send.at[job, sem],
            recv_sem=sum_recv.at[job, sem],
            device_id=shifted(me, axis, step),
            device_id_type=MESH,
        )
        copy.start()
        return copy

    hops = [[] for _ in JOBS]

    def multiply(job):
        a, start, count, order = JOBS[job]
        axis = ORDERS[order][0]
        place, at = room[a]
        if start == 0:
            pair[a].wait_recv()
        pair[3 + job].wait_recv()

        def product(j, _):
            cols = pl.ds(pl.multiple_of(j * 512, 512), 512)
            both = jnp.concatenate([mine[job], lefts[job]], axis=1)
            wide = jnp.concatenate([wides[a, :, cols], rights[a, :, cols]], axis=0)
            weights[place, at + j] = jnp.dot(both, wide, preferred_element_type=jnp.float32).astype(
                jnp.bfloat16
            )
            return 0

        lax.fori_loop(start, start + count, product, 0)
        blocks = pl.ds(at + start, count)
        to = pl.ds(start, count)

        def rows(first_row):
            return weights.at[place, blocks, pl.ds(first_row, 32), :]

        upper, lower = pl.ds(0, 32), pl.ds(32, 32)
        hops[job] = [
            hop(job, axis, 1, 0, rows(128), first.at[a, 2, to, upper, :]),
            hop(job, axis, 3, 1, rows(160), first.at[a, 2, to, lower, :]),
            hop(job, axis, 1, 2, rows(96), first.at[a, 0, to, lower, :]),
            hop(job, axis, 3, 3, rows(192), first.at[a, 1, to, upper, :]),
        ]

    def relay(job):
        a, start, count, order = JOBS[job]
        axis = ORDERS[order][0]
        place, at = room[a]
        blocks = pl.ds(at + start, count)
        to = pl.ds(start, count)
        for step, sem, row, part in ((1, 0, 64, 0), (3, 1, 224, 1)):
            hops[job][sem].wait_recv()
            side = pl.ds(32 * part, 32)

            def add(j, _):
                own = weights[place, at + j, row : row + 32, :].astype(jnp.float32)
                came = first[a, 2, j, 32 * part : 32 * part + 32, :].astype(jnp.float32)
                weights[place, at + j, row : row + 32, :] = (own + came).astype(jnp.bfloat16)
                return 0

            lax.fori_loop(start, start + count, add, 0)
            hops[job].append(
                hop(
                    job,
                    axis,
                    step,
                    4 + part,
                    weights.at[place, blocks, pl.ds(row, 32), :],
                    first.at[a, part, to, side, :],
                )
            )

    multiply(3)
    multiply(4)

    def last(j, _):
        grad = contract_last(grad_low_ref[...], weights[DOWN, j])
        for side in range(2):
            t = 2 * j + side
            wide = grad[:, 128 * side : 128 * side + 128] + factor[t]
            here = pl.ds(pl.multiple_of(t * 256, 256), 256)
            split[here, :] = jnp.concatenate([wide, wide], axis=1).astype(jnp.bfloat16)
        return 0

    lax.fori_loop(0, 13, last, 0)
    relay(3)
    for job in range(3):
        multiply(job)
    relay(4)
    ids = jnp.concatenate([slots_ref[...], jnp.zeros((102, 256), jnp.int32)], axis=0).T
    for t in range(26):
        half = jnp.broadcast_to(ids[:, t : t + 1] >> 10, (256, 128))
        low_side = split[256 * t : 256 * t + 256, 0:128].astype(jnp.float32)
        split[256 * t : 256 * t + 256, 0:128] = jnp.where(half == 0, low_side, 0.0).astype(
            jnp.bfloat16
        )
        split[256 * t : 256 * t + 256, 128:256] = jnp.where(half == 1, low_side, 0.0).astype(
            jnp.bfloat16
        )

    def slots(m, _):
        at = pl.multiple_of(m * 256, 256)
        slot = lax.broadcasted_iota(jnp.int32, (256, 256), 0) + at
        picks = jnp.concatenate(
            [hot(slot == (slots_ref[t : t + 1, :] & 1023)) for t in range(26)], axis=1
        )
        sums = jnp.dot(picks, split[...], preferred_element_type=jnp.float32)
        for side in range(2):
            for block in range(2):
                i = side * 8 + m * 2 + block
                here = pl.ds(pl.multiple_of(i * 128, 128), 128)
                total = sums[128 * block : 128 * block + 128, 128 * side : 128 * side + 128]
                gone = to_column(evict_ref[pl.ds(i, 1), :].astype(jnp.float32))
                cache_ref[here, :] = total * (1.0 - gone)
                sent = total * gone
                upper = poscol[here, :] >> 11
                placed[here, 0:128] = jnp.where(upper == 0, sent, 0.0).astype(jnp.bfloat16)
                placed[here, 128:256] = jnp.where(upper == 1, sent, 0.0).astype(jnp.bfloat16)
        return 0

    lax.fori_loop(0, 4, slots, 0)
    for job in range(3):
        relay(job)
    cache_out = pltpu.make_async_copy(cache_ref, cache_hbm, side_sems.at[1])
    cache_out.start()
    whole = pl.ds(32, 4064)
    pltpu.make_async_copy(val.at[whole, :], val.at[whole, :], val_send).wait()

    def send(j, _):
        at = pl.multiple_of(j * 512, 512)
        place = lax.broadcasted_iota(jnp.int32, (512, 128), 0) + at
        picks = jnp.concatenate(
            [hot(place == (pos[i : i + 1, :] & 2047)) for i in range(16)], axis=1
        )
        sums = jnp.dot(picks, placed[...], preferred_element_type=jnp.float32)
        for side in range(2):
            val[pl.ds(pl.multiple_of(at + 2048 * side, 512), 512), :] = sums[
                :, 128 * side : 128 * side + 128
            ].astype(jnp.bfloat16)
            for more in range(2):
                send_blocks(
                    2 * j + more + 8 * side,
                    side == 0 and more == 0,
                    val,
                    rcv,
                    grad_send,
                    lambda c: grad_recv.at[c],
                )
        return 0

    lax.fori_loop(0, 4, send, 0)
    rcv[0:32, :] = val[0:32, :]

    for job in (3, 4, 0, 1, 2):
        a, start, count, order = JOBS[job]
        place, at = room[a]
        for copy in hops[job][2:6]:
            copy.wait_recv()

        def gather(j, _):
            sums = weights[place, at + j, 0:64, :].astype(jnp.float32)
            for side in range(2):
                sums = sums + first[a, side, j].astype(jnp.float32)
            second_src[a, :, pl.ds(pl.multiple_of(j * 512, 512), 512)] = sums.astype(jnp.bfloat16)
            return 0

        lax.fori_loop(start, start + count, gather, 0)
        cols = pl.ds(start * 512, count * 512)
        for step in (2, 1, 3):
            src = second_src.at[a, pl.ds(16 * step, 16), cols]
            dst = second.at[a, step - 1, :, cols]
            hops[job].append(hop(job, ORDERS[order][1], step, 5 + step, src, dst))

    asked = asked_ref[...]
    wanted = [
        jnp.concatenate(
            [asked[32 * c + 8 * i : 32 * c + 8 * i + 8, 0:32] for i in range(4)], axis=1
        )
        & 2047
        for c in range(4)
    ]
    arrival = (0, 2, 3, 1)

    def arrange(nth):
        c = arrival[nth]
        if c == 0:
            landed = rcv.at[pl.ds(32, 992), :]
        else:
            landed = rcv.at[pl.ds(1024 * c, 1024), :]
        pltpu.make_async_copy(landed, landed, grad_recv.at[c]).wait()
        for i in range(32):
            k = 32 * c + i
            half = qcol[32 * k : 32 * k + 32, :] >> 11
            grad = rcv[32 * k : 32 * k + 32, :].astype(jnp.float32)
            at = 1024 * nth + ((i % 8) * 4 + i // 8) * 32
            spread[at : at + 32, 0:128] = jnp.where(half == 0, grad, 0.0).astype(jnp.bfloat16)
            spread[at : at + 32, 128:256] = jnp.where(half == 1, grad, 0.0).astype(jnp.bfloat16)

    def row_sums(m, first_nth):
        row = lax.broadcasted_iota(jnp.int32, (256, 128), 0) + pl.multiple_of(m * 256, 256)
        picks = jnp.concatenate(
            [
                hot(row == wanted[arrival[nth]][g : g + 1, :])
                for nth in (first_nth, first_nth + 1)
                for g in range(8)
            ],
            axis=1,
        )
        return jnp.dot(
            picks,
            spread[1024 * first_nth : 1024 * first_nth + 2048, :],
            preferred_element_type=jnp.float32,
        )

    def early(m, _):
        sums = row_sums(m, 0)
        factor[2 * m] = sums[:, 0:128]
        factor[2 * m + 1] = sums[:, 128:256]
        return 0

    arrange(0)
    arrange(1)
    lax.fori_loop(0, 8, early, 0)
    arrange(2)
    arrange(3)

    def update(m, _):
        sums = row_sums(m, 2)
        for side in range(2):
            before = factor[2 * m + side]
            for block in range(2):
                i = side * 16 + m * 2 + block
                here = pl.ds(pl.multiple_of(i * 128, 128), 128)
                row_grad = sums[128 * block : 128 * block + 128, 128 * side : 128 * side + 128]
                row_grad = row_grad + before[128 * block : 128 * block + 128]
                acc = to_column(acc_ref[pl.ds(i, 1), :])
                acc = acc + jnp.sum(row_grad * row_grad, axis=1, keepdims=True) * (1.0 / 128.0)
                new_acc_ref[pl.ds(i, 1), :] = acc.T[0:1, :]
                values = rows_ref[here, :].astype(jnp.float32) * to_column(scale_ref[pl.ds(i, 1), :])
                values = values - LEARN_RATE * row_grad / jnp.sqrt(acc)
                top = jnp.max(jnp.abs(values), axis=1, keepdims=True)
                scale = (jnp.broadcast_to(top, (128, 128)) + 1e-06) / QUANT_TOP
                new_scale_ref[pl.ds(i, 1), :] = scale.T[0:1, :]
                new_rows_ref[here, :] = (values / scale).astype(jnp.bfloat16)
        return 0

    lax.fori_loop(0, 4, update, 0)

    for job in (3, 4, 0, 1, 2):
        a, start, count, order = JOBS[job]
        cols = slice(start * 512, (start + count) * 512)
        wide = count * 128
        for copy in hops[job][6:]:
            copy.wait_recv()
        sums = second_src[a, 0:16, cols].astype(jnp.float32)
        for step in range(3):
            sums = sums + second[a, step, :, cols].astype(jnp.float32)
        for step in range(4):
            piece = sums[4 * step : 4 * step + 4, :]
            third_src[a, step, :, start * 128 : start * 128 + wide] = jnp.concatenate(
                [piece[:, wide * i : wide * i + wide] for i in range(4)], axis=0
            ).astype(jnp.bfloat16)
        narrow = pl.ds(start * 128, wide)
        for step in (2, 1, 3):
            src = third_src.at[a, step, :, narrow]
            dst = third.at[a, step - 1, :, narrow]
            hops[job].append(hop(job, ORDERS[order][2], step, 8 + step, src, dst))

    lax.fori_loop(4, 8, update, 0)
    rows_out = pltpu.make_async_copy(new_rows_ref, new_rows_hbm, side_sems.at[2])
    rows_out.start()

    out_refs = (out_down_ref, out_hid_ref, out_up_ref)
    for job in (3, 4, 0, 1, 2):
        a, start, count, order = JOBS[job]
        for copy in hops[job][9:]:
            copy.wait_recv()
        cols = slice(start * 128, (start + count) * 128)
        sums = third_src[a, 0, :, cols].astype(jnp.float32)
        for step in range(3):
            sums = sums + third[a, step, :, cols].astype(jnp.float32)
        sums = sums * (1.0 / 128.0)
        sums = jnp.concatenate([sums[4 * i : 4 * i + 4, :] for i in range(4)], axis=1)
        end = min(3341, (start + count) * 512)
        out_refs[a][:, start * 512 : end] = sums[:, 0 : end - start * 512]

    cache_out.wait()
    rows_out.wait()
    for copy in list(pair.values()) + [copy for some in hops for copy in some]:
        copy.wait_send()
    pltpu.make_async_copy(val.at[whole, :], val.at[whole, :], grad_send).wait()


def store_kernel(*refs):
    held, sems = refs[14:21], refs[21]
    inward = [pltpu.make_async_copy(refs[i], held[i], sems.at[0, i]) for i in range(7)]
    outward = [pltpu.make_async_copy(held[i], refs[7 + i], sems.at[1, i]) for i in range(7)]
    for copy in inward:
        copy.start()
    for i in range(7):
        inward[i].wait()
        outward[i].start()
    for copy in outward:
        copy.wait()


def store(*arrays):
    anywhere = pl.BlockSpec(memory_space=pl.ANY)
    return pl.pallas_call(
        store_kernel,
        name="store",
        out_shape=tuple(jax.ShapeDtypeStruct(a.shape, a.dtype) for a in arrays),
        in_specs=[anywhere] * 7,
        out_specs=(anywhere,) * 7,
        scratch_shapes=[pltpu.VMEM(a.shape, a.dtype) for a in arrays]
        + [pltpu.SemaphoreType.DMA((2, 7))],
        compiler_params=pltpu.CompilerParams(vmem_limit_bytes=62 * 2**20),
    )(*arrays)


def train_step(*operands):
    vmem = pl.BlockSpec(memory_space=pltpu.VMEM)
    anywhere = pl.BlockSpec(memory_space=pl.ANY)
    tail = pl.BlockSpec((128, 512), lambda i: (26, 0), memory_space=pltpu.VMEM)
    bf16, f32, i32 = jnp.bfloat16, jnp.float32, jnp.int32
    dense_out = jax.ShapeDtypeStruct((4, 3341), f32)
    dma = pltpu.SemaphoreType.DMA
    return pl.pallas_call(
        step_kernel,
        name="train_step",
        out_shape=(
            jax.ShapeDtypeStruct((4096, 128), bf16),
            jax.ShapeDtypeStruct((32, 128), f32),
            jax.ShapeDtypeStruct((32, 128), f32),
            jax.ShapeDtypeStruct((2048, 128), f32),
            dense_out,
            dense_out,
            dense_out,
        ),
        grid=(1,),
        in_specs=[vmem] * 6 + [anywhere] + [vmem] * 2 + [anywhere] * 3 + [tail] * 3 + [vmem] * 3,
        out_specs=(anywhere, vmem, vmem, anywhere, vmem, vmem, vmem),
        scratch_shapes=[
            pltpu.VMEM((4096, 128), bf16),
            pltpu.VMEM((4096, 128), bf16),
            pltpu.VMEM((2048, 128), f32),
            pltpu.VMEM((3, 14, 256, 512), bf16),
            pltpu.VMEM((1, 3584), f32),
            pltpu.VMEM((128, 1, 128), i32),
            pltpu.VMEM((128, 1, 128), i32),
            pltpu.VMEM((128, 128), i32),
            pltpu.VMEM((4096, 128), bf16),
            pltpu.VMEM((4096, 128), bf16),
            pltpu.VMEM((4096, 128), bf16),
            pltpu.VMEM((1024, 512), bf16),
            pltpu.VMEM((4096, 128), i32),
            pltpu.VMEM((16, 128), i32),
            pltpu.VMEM((2048, 128), i32),
            pltpu.VMEM((2048, 128), f32),
            pltpu.VMEM((1024, 256), bf16),
            pltpu.VMEM((28, 256, 128), f32),
            pltpu.VMEM((3, 256, 3584), bf16),
            pltpu.VMEM((3, 256, 3584), bf16),
            pltpu.VMEM((256, 512), bf16),
            pltpu.VMEM((256, 512), bf16),
            pltpu.VMEM((256, 512), bf16),
            pltpu.VMEM((6656, 256), bf16),
            pltpu.VMEM((2048, 256), bf16),
            pltpu.VMEM((4096, 256), bf16),
            pltpu.VMEM((5, 256, 256), bf16),
            pltpu.VMEM((5, 256, 256), bf16),
            pltpu.VMEM((5, 256, 256), bf16),
            pltpu.VMEM((3, 3, 7, 64, 512), bf16),
            pltpu.VMEM((3, 64, 3584), bf16),
            pltpu.VMEM((3, 3, 16, 3584), bf16),
            pltpu.VMEM((3, 4, 16, 896), bf16),
            pltpu.VMEM((3, 3, 16, 896), bf16),
            dma((3, 13)),
            dma((3,)),
            dma,
            dma,
            dma,
            dma((4,)),
            dma((8,)),
            dma((8,)),
            dma,
            dma((4,)),
            dma((5, 12)),
            dma((5, 12)),
        ],
        compiler_params=pltpu.CompilerParams(
            collective_id=0, has_side_effects=True, vmem_limit_bytes=62 * 2**20
        ),
    )(*operands)


def on_device(
    dense_feats,
    labels,
    slot_ids,
    needed_owner,
    needed_local,
    evicted,
    table_rows,
    table_scale,
    table_acc,
    cross_down,
    cross_up,
    cross_bias,
    hidden_weight,
    hidden_bias,
    out_weight,
):
    up_t = cross_up.T
    results = train_step(
        needed_owner.reshape(1, 2048),
        needed_local.reshape(1, 2048),
        slot_ids.T,
        dense_feats.T,
        labels.reshape(1, 256),
        evicted.reshape(16, 128),
        table_rows,
        table_scale.reshape(32, 128),
        table_acc.reshape(32, 128),
        cross_down,
        up_t,
        hidden_weight,
        cross_down,
        up_t,
        hidden_weight,
        cross_bias,
        hidden_bias.reshape(1, 512),
        out_weight,
    )
    new_rows, new_scale, new_acc, cache, grad_down, grad_hidden, grad_up = store(*results)
    return (
        new_rows,
        new_scale.reshape(4096),
        new_acc.reshape(4096),
        cache,
        grad_down,
        grad_hidden,
        grad_up,
    )


def solution(mesh):
    placed = (
        P(("hst", "chip"), None),
        P(("hst", "chip")),
        P(("hst", "chip"), None),
        P(("hst", "chip"), None),
        P(("hst", "chip")),
        P(("hst", "chip")),
        P(("hst", "chip"), None),
        P(("hst", "chip")),
        P(("hst", "chip")),
        P(),
        P(),
        P(),
        P(),
        P(),
        P(),
    )
    return jax.shard_map(
        on_device,
        mesh=mesh,
        in_specs=placed,
        out_specs=(
            P(("hst", "chip"), None),
            P(("hst", "chip")),
            P(("hst", "chip")),
            P(("hst", "chip"), None),
            P(("hst", "chip"), None),
            P(("hst", "chip"), None),
            P(("hst", "chip"), None),
        ),
        check_vma=False,
    )
```
